512 devices in a mesh: cube: 512 (over x, y, z, core).
Axes of the slice: x: 4, y: 4, z: 16, core: 2. Of those that a mesh axis runs over, the one named last changes fastest.
Arguments:
- points: float32 [8192, 3, 512], P('cube'), may hold values from -1 to 1
- charges: float32 [8192, 4, 512], P('cube'), may hold values from -0.15 to 0.15
- leaf_density: float32 [8192, 4, 296], P('cube'), may hold values from -6 to 6
- leaf_octant: int32 [8192], P('cube'), may hold values from 0 to 511, as said below
- user_lists: int32 [512, 2, 4], P('cube'), may hold values from 0 to 15
- near_leaves: int32 [8192, 4], P('cube'), may hold values from 0 to 23
- near_codes: int32 [8192, 4], P('cube'), may hold values from 0 to 25
- upward_map: float32 [296, 296], replicated, may hold values from -0.09375 to 0.09375
- lower_map: float32 [296, 296], replicated, may hold values from -0.25 to 0.25
- upper_map: float32 [296, 296], replicated, may hold values from -0.25 to 0.25
- downward_map: float32 [296, 296], replicated, may hold values from -0.375 to 0.375
Outputs:
- potential: float32 [8192, 4, 512], P('cube')
The draws below stay inside these ranges and needn't reach their ends.
Inputs may be any that keep to these rules, and one draw needn't show every extreme that they name: user_lists[d, 0] names leaf boxes of partition d - 1 and user_lists[d, 1] of partition d + 1, as indices within that partition; entries of missing partitions are unused. `near_leaves`: rows of the near set: own boxes first, then the 4 read from below, then the 4 read from above. `near_codes`: one of the 26 neighbour directions. `leaf_octant`: any shared octant; some leaf boxes of every partition lie in arbitrary octants, which may be held anywhere along the axis.
All inputs are finite; a program needn't handle non-finite values.
Results may differ from the reference program's by a relative error of at most 0.0003.
Values sent between devices are 32-bit elements; how exact they have to be, the bound alone decides.
A program may use at most 64 MiB of HBM per device.

```python
import math
import jax
import jax.numpy as jnp
import numpy as np
from jax import lax

EQ_ORDER = 8
S = 296
Q = 4
P_SIZE = 512
K = 4
LB = 16
UH = 4
SHARED = 512
LEAVES = 8192
N_CUBE = 512


def draw_points(key, part):
    key = jax.random.fold_in(key, 7)
    side = jax.random.uniform(jax.random.fold_in(key, 13), (LEAVES, 3, P_SIZE), jnp.float32)
    depth = jax.random.uniform(jax.random.fold_in(key, 29), (LEAVES, 3, P_SIZE), jnp.float32)
    direction = jnp.where(side < 0.5, -1.0, 1.0).astype(jnp.float32)
    magnitude = 1.0 - depth * depth
    return (direction * magnitude).astype(jnp.float32)


def draw_leaf_octant(key, part):
    key = jax.random.fold_in(key, 5)
    key_low = jax.random.fold_in(key, 11)
    key_high = jax.random.fold_in(key, 23)
    key_first = jax.random.fold_in(key, 37)
    key_middle = jax.random.fold_in(key, 41)
    key_chosen = jax.random.fold_in(key, 53)
    spill_low = jax.random.randint(key_low, (N_CUBE, 1), 0, LB // 4 + 1)
    spill_high = jax.random.randint(key_high, (N_CUBE, 1), 0, LB // 4 + 1)
    slot_index = jnp.arange(LB, dtype=jnp.int32)[None, :]
    part_index = jnp.arange(N_CUBE, dtype=jnp.int32)[:, None]
    lower_slot = ((slot_index >= 1) & (slot_index < 1 + spill_low)).astype(jnp.int32)
    upper_slot = (slot_index >= LB - spill_high).astype(jnp.int32)
    octant = part_index - lower_slot + upper_slot
    octant = jnp.clip(octant, 0, SHARED - 1)
    first_pick = jax.random.randint(key_first, (N_CUBE, 1), 0, SHARED)
    middle_pick = jax.random.randint(key_middle, (N_CUBE, 1), 0, SHARED)
    chosen_part = jax.random.randint(key_chosen, (), 0, N_CUBE)
    opposite = (part_index + SHARED // 2) % SHARED
    first_pick = jnp.where(part_index == chosen_part, opposite, first_pick)
    octant = jnp.where(slot_index == LB // 2, middle_pick, octant)
    octant = jnp.where(slot_index == 0, first_pick, octant)
    return octant.reshape(LB * N_CUBE).astype(jnp.int32)


def place_ends(values, stream_key, least, top_value):
    dims = values.shape
    index_at = [jax.random.randint(jax.random.fold_in(stream_key, axis), (), 0, dims[axis]) for axis in range(len(dims))]
    values = values.at[tuple(index_at)].set(least)
    longest = dims.index(max(dims))
    index_at[longest] = (index_at[longest] + 1) % dims[longest]
    return values.at[tuple(index_at)].set(top_value)


def levels(stream_key, extent, pieces, smallest, high):
    factor_of = 1.0
    for axis_at, shards_of in pieces:
        steps = jax.random.uniform(jax.random.fold_in(jax.random.fold_in(stream_key, 6), axis_at), (shards_of,), jnp.float32, smallest / len(pieces), high / len(pieces))
        factor_of = factor_of * jnp.repeat(jnp.exp(steps), extent[axis_at] // shards_of).reshape((-1,) + (1,) * (len(extent) - 1 - axis_at))
    return factor_of


def scatter_about(rng, extent, width, limit, cuts=(), held_as=jnp.bfloat16):
    loudness = levels(rng, extent, cuts, -0.22, 0.18) if cuts else 1.0
    drawn = jax.random.normal(rng, extent, jnp.float32) * width * loudness
    return jnp.minimum(jnp.maximum(drawn, -limit), limit).astype(held_as)


def setup_inputs(seed: int = 0) -> dict:
    key_list = jax.random.split(jax.random.key(seed), 12)
    return {
        "points": draw_points(jax.random.fold_in(key_list[11], 71), 0),
        "charges": scatter_about(key_list[1], (LEAVES, Q, P_SIZE), 0.025, 0.15, ((0, 512),), jnp.float32),
        "leaf_density": scatter_about(key_list[2], (LEAVES, Q, S), 1.0, 6.0, ((0, 512),), jnp.float32),
        "leaf_octant": draw_leaf_octant(jax.random.fold_in(key_list[11], 71), 0),
        "user_lists": place_ends(jax.random.randint(key_list[4], (N_CUBE, 2, UH), 0, LB), jax.random.fold_in(key_list[4], 1), 0, LB - 1).astype(jnp.int32),
        "near_leaves": place_ends(jax.random.randint(key_list[5], (LEAVES, K), 0, LB + 2 * UH), jax.random.fold_in(key_list[5], 1), 0, (LB + 2 * UH) - 1).astype(jnp.int32),
        "near_codes": place_ends(jax.random.randint(key_list[6], (LEAVES, K), 0, 26), jax.random.fold_in(key_list[6], 1), 0, 25).astype(jnp.int32),
        "upward_map": scatter_about(key_list[7], (S, S), (S * LB) ** -0.5, 0.09375, (), jnp.float32),
        "lower_map": scatter_about(key_list[8], (S, S), (2 * S) ** -0.5, 0.25, (), jnp.float32),
        "upper_map": scatter_about(key_list[9], (S, S), (2 * S) ** -0.5, 0.25, (), jnp.float32),
        "downward_map": scatter_about(key_list[10], (S, S), S ** -0.5, 0.375, (), jnp.float32),
    }


inv_four_pi = 1.0 / (4.0 * math.pi)
soften = 0.01

def surface_table():
    spacing = np.linspace(-1.0, 1.0, EQ_ORDER)
    mesh_x, mesh_y, mesh_z = np.meshgrid(spacing, spacing, spacing, indexing='ij')
    lattice = np.stack([mesh_x.ravel(), mesh_y.ravel(), mesh_z.ravel()], 0)
    on_boundary = np.max(np.abs(lattice), axis=0) > 0.999
    return lattice[:, on_boundary] * 2.95

def kernel(targets, sources):
    separation = targets[..., :, :, None] - sources[..., :, None, :]
    return inv_four_pi / jnp.sqrt(lax.optimization_barrier(jnp.sum(separation * separation, axis=-3)) + soften)

def direction_offsets(codes):
    shifted = codes + (codes >= 13).astype(jnp.int32)
    parts_xyz = jnp.stack([shifted // 9 - 1, shifted // 3 % 3 - 1, shifted % 3 - 1], -1)
    return 2.0 * parts_xyz.astype(jnp.float32)

def near_and_far(targets, own_charges, set_points, set_charges, local_block, neighbours, codes, surface):
    highest = lax.Precision.HIGHEST
    totals = jnp.einsum('lps,lqs->lqp', kernel(targets, targets), own_charges, precision=highest)
    offsets = direction_offsets(codes)
    for slot_index in range(neighbours.shape[1]):
        rows = neighbours[:, slot_index]
        sources = set_points[rows] + offsets[:, slot_index, :, None]
        totals = totals + jnp.einsum('lps,lqs->lqp', kernel(targets, sources), set_charges[rows], precision=highest)
    far_field = jnp.einsum('lps,lqs->lqp', kernel(targets, surface), local_block, precision=highest)
    return far_field + totals

def reference(points, charges, leaf_density, leaf_octant, user_lists, near_leaves, near_codes, upward_map, lower_map, upper_map, downward_map):
    highest = lax.Precision.HIGHEST
    leaf_part = jnp.einsum('lqs,st->lqt', leaf_density, upward_map, precision=highest)
    octant_density = jax.ops.segment_sum(leaf_part, leaf_octant, num_segments=SHARED)
    zero_block = jnp.zeros((1, Q, S), jnp.float32)
    octant_lower = jnp.concatenate([zero_block, octant_density[:-1]], 0)
    octant_upper = jnp.concatenate([octant_density[1:], zero_block], 0)
    octant_local = jnp.einsum('oqs,st->oqt', octant_lower, lower_map, precision=highest) + jnp.einsum('oqs,st->oqt', octant_upper, upper_map, precision=highest)
    leaf_local = jnp.einsum('lqs,st->lqt', octant_local[leaf_octant], downward_map, precision=highest)
    surface = jnp.asarray(surface_table(), jnp.float32)
    leaf_points = points.reshape(N_CUBE, LB, 3, P_SIZE)
    leaf_charges = charges.reshape(N_CUBE, LB, Q, P_SIZE)
    local_parts = leaf_local.reshape(N_CUBE, LB, Q, S)
    near_parts = near_leaves.reshape(N_CUBE, LB, K)
    code_parts = near_codes.reshape(N_CUBE, LB, K)

    def one_device(device_index):
        lower_index = jnp.maximum(device_index - 1, 0)
        upper_index = jnp.minimum(device_index + 1, N_CUBE - 1)
        lower_present = (device_index > 0).astype(points.dtype)
        upper_present = (device_index < N_CUBE - 1).astype(points.dtype)
        lower_rows = user_lists[device_index, 0]
        upper_rows = user_lists[device_index, 1]
        own_points = leaf_points[device_index]
        own_charges = leaf_charges[device_index]
        set_points = jnp.concatenate([own_points, leaf_points[lower_index][lower_rows] * lower_present, leaf_points[upper_index][upper_rows] * upper_present], 0)
        set_charges = jnp.concatenate([own_charges, leaf_charges[lower_index][lower_rows] * lower_present, leaf_charges[upper_index][upper_rows] * upper_present], 0)
        return near_and_far(own_points, own_charges, set_points, set_charges, local_parts[device_index], near_parts[device_index], code_parts[device_index], surface)
    result = lax.map(one_device, jnp.arange(N_CUBE, dtype=jnp.int32))
    return result.reshape(LEAVES, Q, P_SIZE)
```

```python
import functools
import math

import jax
import jax.numpy as jnp
import numpy as np
from jax import lax
from jax.experimental import pallas as pl
from jax.experimental.pallas import tpu as pltpu
from jax.sharding import PartitionSpec as P

EQ_ORDER = 8
INV_FOUR_PI = 1.0 / (4.0 * math.pi)
SOFTEN = 0.01
LB = 16
UH = 4
K = 4
Q = 4
S = 296
SP = 384
PTS = 512
FAR = 304
ROWS = LB * Q
MESH = pl.DeviceIdType.MESH
F32 = jnp.float32
BF16 = jnp.bfloat16
NX, NY, NZ = 4, 4, 16
NG = 4


def surface_table():
    spacing = np.linspace(-1.0, 1.0, EQ_ORDER)
    mesh_x, mesh_y, mesh_z = np.meshgrid(spacing, spacing, spacing, indexing="ij")
    lattice = np.stack([mesh_x.ravel(), mesh_y.ravel(), mesh_z.ravel()], 0)
    on_boundary = np.max(np.abs(lattice), axis=0) > 0.999
    return lattice[:, on_boundary] * 2.95


def split3(v):
    a = v.astype(BF16).astype(F32)
    r = v - a
    b = r.astype(BF16).astype(F32)
    return a, b, r - b


def source_features(p, row):
    nsq = jnp.sum(p * p, axis=0, keepdims=True)
    u = jnp.where(row == 3, nsq, jnp.where(row == 4, 1.0, p))
    a, b, c = split3(u)
    return jnp.concatenate([a, a, b, b, a, c], axis=0)


def target_features(t, row):
    nsq = jnp.sum(t * t, axis=0, keepdims=True) + SOFTEN
    v = jnp.where(row == 3, 1.0, jnp.where(row == 4, nsq, -2.0 * t))
    a, b, c = split3(v)
    return jnp.concatenate([a, b, a, b, c, a], axis=0).astype(BF16)


def surface_features():
    pts = np.zeros((8, FAR), np.float32)
    pts[:3, :S] = surface_table().astype(np.float32)
    pts[:3, S:] = pts[:3, :1]
    u = pts.copy()
    u[3] = np.sum(pts * pts, axis=0)
    u[4] = 1.0
    a = u.astype(jnp.bfloat16).astype(np.float32)
    b = (u - a).astype(jnp.bfloat16).astype(np.float32)
    c = u - a - b
    return np.concatenate([a, a, b, b, a, c], axis=0).T.astype(jnp.bfloat16)


def pair_sum(feat, ft, weights):
    r2 = jnp.dot(feat, ft, preferred_element_type=F32)
    g = lax.rsqrt(r2)
    hi = g.astype(BF16)
    lo = (g - hi.astype(F32)).astype(BF16)
    return jnp.dot(weights, hi, preferred_element_type=F32) + jnp.dot(
        weights, lo, preferred_element_type=F32
    )


OCT, USER, NEAR, CODE = 0, LB, LB + 2 * UH, LB + 2 * UH + LB * K
N_META = CODE + LB * K


def kernel(
    meta, pts, ch, dens, up, low, upp, down, fsurf,
    out,
    xp, fs, cw, hp, hc, near, rbuf, p1, qb, p2, zb, table, sel, cfar,
    halo_s, halo_r, core_s, core_r, a_s, a_r, b_s, b_r, z_s, z_r,
    gz_s, gz_r, gb_s, gb_r, ga_s, ga_r, gc_s, gc_r,
):
    me = lax.axis_index("cube")
    count = 2 * NX * NY * NZ
    core = me % 2
    z = (me // 2) % NZ
    y = (me // (2 * NZ)) % NY
    x = me // (2 * NZ * NY)
    stride_x, stride_y = 2 * NZ * NY, 2 * NZ
    stride_a = stride_x * (1 - core) + stride_y * core
    stride_b = stride_y * (1 - core) + stride_x * core
    a = x * (1 - core) + y * core
    b = y * (1 - core) + x * core
    a_partner = y * (1 - core) + x * core
    partner = me + 1 - 2 * core
    oct_a = core * (NG * NG * NZ) + a * (NG * NZ)
    oct_b = oct_a + b * NZ
    oct_z = oct_b + z

    def peer_a(i):
        return me + ((a + i) % NG - a) * stride_a

    def peer_b(i):
        return me + ((b + i) % NG - b) * stride_b

    def peer_z(i):
        return me + ((z + i) % NZ - z) * 2

    def send(src, dst, s, r, dev):
        return pltpu.make_async_remote_copy(
            src_ref=src, dst_ref=dst, send_sem=s, recv_sem=r, device_id=(dev,), device_id_type=MESH
        )

    row8 = lax.broadcasted_iota(jnp.int32, (8, PTS), 0)

    barrier = pltpu.get_barrier_semaphore()

    def greet(dev):
        pl.semaphore_signal(barrier, inc=1, device_id=(dev,), device_id_type=MESH)

    greet(partner)
    for i in range(1, NG):
        greet(peer_a(i))
        greet(peer_b(i))

    def greet_z(i, _):
        greet(peer_z(i))
        return 0

    lax.fori_loop(1, NZ, greet_z, 0)
    n_greet = 1 + 2 * (NG - 1) + NZ - 1

    @pl.when(me > 0)
    def _():
        greet(me - 1)

    @pl.when(me < count - 1)
    def _():
        greet(me + 1)

    mine = a * 2 + core
    rbuf[mine] = jnp.zeros((ROWS + 8, SP), F32)
    for l in range(LB):
        rbuf[mine, Q * l : Q * l + Q, 0:S] = dens[l]
    lane = lax.broadcasted_iota(jnp.int32, (8, SP), 1) % ROWS
    keys = jnp.zeros((8, SP), jnp.int32)
    for l in range(LB):
        keys = jnp.where(lane // Q == l, meta[OCT + l], keys)
    rbuf[mine, ROWS : ROWS + 8, :] = (keys * Q + lane % Q).astype(F32)

    def prep(n, p, q):
        fs[n] = source_features(p, row8).T.astype(BF16)
        hi = q.astype(BF16).astype(F32)
        lo = q - hi
        cw[n] = jnp.concatenate([hi + pltpu.roll(lo, 4, 0), jnp.zeros((8, PTS), F32)], axis=0).astype(BF16)

    xp[...] = jnp.zeros(xp.shape, F32)

    def prep_own(n, _):
        xp[n, 0:3, :] = pts[n]
        xp[LB, 0:4, :] = ch[n] * INV_FOUR_PI
        prep(n, xp[n], xp[LB])
        return 0

    n_wait = n_greet + (me + count - 1) // count + (2 * count - 2 - me) // count
    pl.semaphore_wait(barrier, n_wait)

    def halo(i):
        dev = me + 1 - 2 * i
        return (
            send(pts, hp.at[i], halo_s.at[i], halo_r.at[i], dev),
            send(ch, hc.at[i], halo_s.at[2 + i], halo_r.at[2 + i], dev),
        )

    core_out = send(rbuf.at[mine], rbuf.at[a_partner * 2 + core], core_s, core_r, partner)
    core_in = send(rbuf.at[mine], rbuf.at[a * 2 + 1 - core], core_s, core_r, partner)
    core_out.start()

    @pl.when(me < count - 1)
    def _():
        for c in halo(0):
            c.start()

    @pl.when(me > 0)
    def _():
        for c in halo(1):
            c.start()

    lax.fori_loop(0, LB, prep_own, 0)

    def a_copy(i, at):
        return send(rbuf.at[pl.ds(at * 2, 2)], rbuf.at[pl.ds(at * 2, 2)], a_s.at[i], a_r.at[i], peer_a(i))

    def b_copy(i, chunk, at):
        return send(p1.at[pl.ds(chunk * NZ * Q, NZ * Q)], qb.at[at], b_s.at[i], b_r.at[i], peer_b(i))

    def z_copy(i, chunk, at):
        return send(p2.at[chunk], zb.at[at], z_s.at[i], z_r.at[i], peer_z(i))

    def gz_copy(i, o):
        return send(table.at[o], table.at[o], gz_s.at[i], gz_r.at[i], peer_z(i))

    def gb_copy(i, o):
        return send(table.at[pl.ds(o, NZ)], table.at[pl.ds(o, NZ)], gb_s.at[i], gb_r.at[i], peer_b(i))

    def ga_copy(i, o):
        return send(
            table.at[pl.ds(o, NG * NZ)], table.at[pl.ds(o, NG * NZ)], ga_s.at[i], ga_r.at[i], peer_a(i)
        )

    def gc_copy(c):
        half = NG * NG * NZ
        return send(table.at[pl.ds(c * half, half)], table.at[pl.ds(c * half, half)], gc_s, gc_r, partner)

    def step_a():
        core_in.wait_recv()
        for i in range(1, NG):
            a_copy(i, a).start()

    def step_b():
        for i in range(1, NG):
            a_copy(i, (a + NG - i) % NG).wait_recv()
        rows = lax.broadcasted_iota(jnp.int32, (NG * NZ * Q, 3 * ROWS), 0) + oct_a * Q
        rows = rows.astype(F32)
        p1[...] = jnp.zeros(p1.shape, F32)

        def add(j, _):
            member = jnp.where(rows == rbuf[j, ROWS : ROWS + 1, 0 : 3 * ROWS], 1.0, 0.0).astype(BF16)
            parts = jnp.concatenate(split3(rbuf[j, 0:ROWS, :]), axis=0).astype(BF16)
            p1[...] += jnp.dot(member, parts, preferred_element_type=F32)
            return 0

        lax.fori_loop(0, 2 * NG, add, 0)
        for i in range(1, NG):
            b_copy(i, (b + i) % NG, b).start()

    def step_z():
        total = p1[pl.ds(pl.multiple_of(b * NZ * Q, 8), NZ * Q), :]
        for i in range(1, NG):
            at = (b + NG - i) % NG
            b_copy(i, at, at).wait_recv()
            total = total + qb[at]
        for j in range(NZ):
            p2[j] = total[Q * j : Q * j + Q, :]

        def go(i, _):
            z_copy(i, (z + i) % NZ, z).start()
            return 0

        lax.fori_loop(1, NZ, go, 0)

    def step_gz():
        def take(i, total):
            at = (z + NZ - i) % NZ
            z_copy(i, at, at).wait_recv()
            return total + zb[at]

        table[oct_z] = lax.fori_loop(1, NZ, take, p2[z])

        def go(i, _):
            gz_copy(i, oct_z).start()
            return 0

        lax.fori_loop(1, NZ, go, 0)

    def step_gb():
        def take(i, _):
            gz_copy(i, oct_b + (z + NZ - i) % NZ).wait_recv()
            return 0

        lax.fori_loop(1, NZ, take, 0)
        for i in range(1, NG):
            gb_copy(i, oct_b).start()

    def step_ga():
        for i in range(1, NG):
            gb_copy(i, oct_a + (b + NG - i) % NG * NZ).wait_recv()
        for i in range(1, NG):
            ga_copy(i, oct_a).start()

    def step_gc():
        for i in range(1, NG):
            ga_copy(i, core * (NG * NG * NZ) + (a + NG - i) % NG * (NG * NZ)).wait_recv()
        gc_copy(core).start()

    def own_leaf(l, _):
        near[l] = pair_sum(fs[l], target_features(xp[l], row8), cw[l])

        @pl.when(l == OWN_AT[0])
        def _():
            step_a()

        @pl.when(l == OWN_AT[1])
        def _():
            step_b()

        return 0

    lax.fori_loop(0, LB, own_leaf, 0)

    for i in range(2):
        present = me > 0 if i == 0 else me < count - 1

        @pl.when(present)
        def _():
            for c in halo(i):
                c.wait_recv()

        @pl.when(jnp.logical_not(present))
        def _():
            hp[i] = jnp.zeros(hp.shape[1:], F32)
            hc[i] = jnp.zeros(hc.shape[1:], F32)

    for i in range(2):

        def prep_halo(j, _):
            n = meta[USER + i * UH + j]
            xp[LB + 1, 0:3, :] = hp[i, n]
            xp[LB, 0:4, :] = hc[i, n] * INV_FOUR_PI
            prep(LB + i * UH + j, xp[LB + 1], xp[LB])
            return 0

        lax.fori_loop(0, UH, prep_halo, 0)

    def near_leaf(l, _):
        acc = near[l]
        box = xp[l]
        for k in range(K):
            n = meta[NEAR + l * K + k]
            code = meta[CODE + l * K + k]
            code = jnp.where(code >= 13, code + 1, code)
            ox = (2 * (code // 9 - 1)).astype(F32)
            oy = (2 * ((code // 3) % 3 - 1)).astype(F32)
            oz = (2 * (code % 3 - 1)).astype(F32)
            off = jnp.where(row8 == 0, ox, jnp.where(row8 == 1, oy, jnp.where(row8 == 2, oz, 0.0)))
            acc = acc + pair_sum(fs[n], target_features(box - off, row8), cw[n])
        near[l] = acc
        for at, step in zip(NEAR_AT, (step_z, step_gz, step_gb, step_ga, step_gc)):

            @pl.when(l == at)
            def _():
                step()

        return 0

    lax.fori_loop(0, LB, near_leaf, 0)

    gc_copy(1 - core).wait_recv()
    n_oct = NX * NY * NZ * 2
    for l in range(LB):
        o = meta[OCT + l]
        below = jnp.where(o > 0, 1.0, 0.0).astype(F32)
        above = jnp.where(o < n_oct - 1, 1.0, 0.0).astype(F32)
        sel[Q * l : Q * l + Q, :] = table[jnp.maximum(o - 1, 0)] * below
        sel[ROWS + Q * l : ROWS + Q * l + Q, :] = table[jnp.minimum(o + 1, n_oct - 1)] * above
    highest = lax.Precision.HIGHEST
    t = jnp.dot(sel[:, 0:S], up[...], precision=highest, preferred_element_type=F32)
    w = jnp.dot(t[0:ROWS], low[...], precision=highest, preferred_element_type=F32) + jnp.dot(
        t[ROWS:], upp[...], precision=highest, preferred_element_type=F32
    )
    w = jnp.dot(w, down[...], precision=highest, preferred_element_type=F32) * INV_FOUR_PI
    hi = w.astype(BF16).astype(F32)
    lo = w - hi
    cfar[...] = jnp.zeros(cfar.shape, BF16)
    for t in range(LB // 2):
        pair = jnp.concatenate([hi[8 * t : 8 * t + 8], lo[8 * t : 8 * t + 8]], axis=0)
        cfar[t, :, 0:S] = pair.astype(BF16)

    def far_pair(t, _):
        for h in range(2):
            l = 2 * t + h
            far = pair_sum(fsurf[...], target_features(xp[l], row8), cfar[t, :, 0:FAR])
            far = far[0:8] + far[8:16]
            out[l] = far[4 * h : 4 * h + 4] + near[l, 0:4, :] + near[l, 4:8, :]
        return 0

    lax.fori_loop(0, LB // 2, far_pair, 0)

    core_out.wait_send()

    @pl.when(me < count - 1)
    def _():
        for c in halo(0):
            c.wait_send()

    @pl.when(me > 0)
    def _():
        for c in halo(1):
            c.wait_send()

    for i in range(1, NG):
        a_copy(i, a).wait_send()
        b_copy(i, (b + i) % NG, b).wait_send()
        gb_copy(i, oct_b).wait_send()
        ga_copy(i, oct_a).wait_send()

    def sent_z(i, _):
        z_copy(i, (z + i) % NZ, z).wait_send()
        gz_copy(i, oct_z).wait_send()
        return 0

    lax.fori_loop(1, NZ, sent_z, 0)
    gc_copy(core).wait_send()


OWN_AT = (4, 12)
NEAR_AT = (0, 2, 4, 7, 13)


def body(points, charges, leaf_density, leaf_octant, user_lists, near_leaves, near_codes,
         upward_map, lower_map, upper_map, downward_map):
    meta = jnp.concatenate(
        [leaf_octant, user_lists.reshape(-1), near_leaves.reshape(-1), near_codes.reshape(-1)]
    )
    vmem = pl.BlockSpec(memory_space=pltpu.VMEM)
    dma = pltpu.SemaphoreType.DMA
    n_oct = 2 * NX * NY * NZ
    return pl.pallas_call(
        kernel,
        out_shape=jax.ShapeDtypeStruct((LB, Q, PTS), F32),
        in_specs=[pl.BlockSpec(memory_space=pltpu.SMEM)] + [vmem] * 8,
        out_specs=vmem,
        scratch_shapes=[
            pltpu.VMEM((LB + 2, 8, PTS), F32),
            pltpu.VMEM((LB + 2 * UH, PTS, 48), BF16),
            pltpu.VMEM((LB + 2 * UH, 16, PTS), BF16),
            pltpu.VMEM((2, LB, 3, PTS), F32),
            pltpu.VMEM((2, LB, Q, PTS), F32),
            pltpu.VMEM((LB, 16, PTS), F32),
            pltpu.VMEM((2 * NG, ROWS + 8, SP), F32),
            pltpu.VMEM((NG * NZ * Q, SP), F32),
            pltpu.VMEM((NG, NZ * Q, SP), F32),
            pltpu.VMEM((NZ, Q, SP), F32),
            pltpu.VMEM((NZ, Q, SP), F32),
            pltpu.VMEM((n_oct, Q, SP), F32),
            pltpu.VMEM((2 * ROWS, SP), F32),
            pltpu.VMEM((LB // 2, 16, SP), BF16),
            dma((4,)), dma((4,)), dma, dma,
            dma((NG,)), dma((NG,)), dma((NG,)), dma((NG,)), dma((NZ,)), dma((NZ,)),
            dma((NZ,)), dma((NZ,)), dma((NG,)), dma((NG,)), dma((NG,)), dma((NG,)), dma, dma,
        ],
        compiler_params=pltpu.CompilerParams(
            collective_id=0, has_side_effects=True, vmem_limit_bytes=50 * 2**20
        ),
    )(
        meta, points, charges, leaf_density, upward_map, lower_map, upper_map, downward_map,
        jnp.asarray(surface_features()),
    )


def solution(mesh):
    in_specs = (
        P("cube", None, None),
        P("cube", None, None),
        P("cube", None, None),
        P("cube"),
        P("cube", None, None),
        P("cube", None),
        P("cube", None),
        P(),
        P(),
        P(),
        P(),
    )
    return jax.shard_map(
        body, mesh=mesh, in_specs=in_specs, out_specs=P("cube", None, None), check_vma=False
    )
```

```python
import functools
import math

import jax
import jax.numpy as jnp
import numpy as np
from jax import lax
from jax.experimental import pallas as pl
from jax.experimental.pallas import tpu as pltpu
from jax.sharding import PartitionSpec as P

EQ_ORDER = 8
INV_FOUR_PI = 1.0 / (4.0 * math.pi)
SOFTEN = 0.01
LB = 16
UH = 4
K = 4
Q = 4
S = 296
SP = 384
PTS = 512
FAR = 304
ROWS = LB * Q
MESH = pl.DeviceIdType.MESH
F32 = jnp.float32
BF16 = jnp.bfloat16
NX, NY, NZ = 4, 4, 16
NG = 4


def surface_table():
    spacing = np.linspace(-1.0, 1.0, EQ_ORDER)
    mesh_x, mesh_y, mesh_z = np.meshgrid(spacing, spacing, spacing, indexing="ij")
    lattice = np.stack([mesh_x.ravel(), mesh_y.ravel(), mesh_z.ravel()], 0)
    on_boundary = np.max(np.abs(lattice), axis=0) > 0.999
    return lattice[:, on_boundary] * 2.95


def split3(v):
    a = v.astype(BF16).astype(F32)
    r = v - a
    b = r.astype(BF16).astype(F32)
    return a, b, r - b


def source_features(p, row):
    nsq = jnp.sum(p * p, axis=0, keepdims=True)
    u = jnp.where(row == 3, nsq, jnp.where(row == 4, 1.0, p))
    a, b, c = split3(u)
    return jnp.concatenate([a, a, b, b, a, c], axis=0)


def target_features(t, row):
    nsq = jnp.sum(t * t, axis=0, keepdims=True) + SOFTEN
    v = jnp.where(row == 3, 1.0, jnp.where(row == 4, nsq, -2.0 * t))
    a, b, c = split3(v)
    return jnp.concatenate([a, b, a, b, c, a], axis=0).astype(BF16)


def surface_features():
    pts = np.zeros((8, FAR), np.float32)
    pts[:3, :S] = surface_table().astype(np.float32)
    pts[:3, S:] = pts[:3, :1]
    u = pts.copy()
    u[3] = np.sum(pts * pts, axis=0)
    u[4] = 1.0
    a = u.astype(jnp.bfloat16).astype(np.float32)
    b = (u - a).astype(jnp.bfloat16).astype(np.float32)
    c = u - a - b
    return np.ascontiguousarray(np.concatenate([a, a, b, b, a, c], axis=0).T)


def green(feat, ft):
    g = lax.rsqrt(jnp.dot(feat, ft, preferred_element_type=F32))
    hi = g.astype(BF16)
    return hi, (g - hi.astype(F32)).astype(BF16)


def pair_sum(feat, ft, weights):
    parts = []
    for at in range(0, PTS, 256):
        hi, lo = green(feat, ft[:, at : at + 256])
        parts.append(
            jnp.dot(weights, hi, preferred_element_type=F32)
            + jnp.dot(weights, lo, preferred_element_type=F32)
        )
    return jnp.concatenate(parts, axis=1)


def split2(v):
    hi = v.astype(BF16)
    return hi, (v - hi.astype(F32)).astype(BF16)


def dot3(x, w_hi, w_lo):
    hi, lo = split2(x)
    n = x.shape[0]
    both = jnp.concatenate([hi, lo], axis=0)
    r = jnp.dot(both, w_hi, preferred_element_type=F32)
    return r[:n] + r[n:] + jnp.dot(hi, w_lo, preferred_element_type=F32)


def kernel(
    octs, users, nears, codes, pts_in, ch_in, dens_in, up_in, low_in, upp_in, down_in, surf_in,
    out,
    pts, ch, dens, maps, surf, maps_hi, maps_lo, fsurf,
    xp, fs, cw, hp, hc, near, rbuf, p1, qb, p2, zb, gz, g2, wb, sbuf, vbuf, tot, ebuf, cfar, gh, gl,
    near_s, far_s, load_s, halo_s, halo_r, core_s, core_r, am_s, am_r, ao_s, ao_r, b_s, b_r, z_s, z_r,
    gz_s, gz_r, gb_s, gb_r, v_s, v_r, e_s, e_r,
):
    me = lax.axis_index("cube")
    count = 2 * NX * NY * NZ
    core = me % 2
    z = (me // 2) % NZ
    y = (me // (2 * NZ)) % NY
    x = me // (2 * NZ * NY)
    stride_x, stride_y = 2 * NZ * NY, 2 * NZ
    stride_a = stride_x * (1 - core) + stride_y * core
    stride_b = stride_y * (1 - core) + stride_x * core
    a = x * (1 - core) + y * core
    b = y * (1 - core) + x * core
    a_partner = y * (1 - core) + x * core
    partner = me + 1 - 2 * core
    oct_a = core * (NG * NG * NZ) + a * (NG * NZ)

    def peer_a(i):
        return me + ((a + i) % NG - a) * stride_a

    def peer_b(i):
        return me + ((b + i) % NG - b) * stride_b

    def peer_z(i):
        return me + ((z + i) % NZ - z) * 2

    def send(src, dst, s, r, dev):
        return pltpu.make_async_remote_copy(
            src_ref=src, dst_ref=dst, send_sem=s, recv_sem=r, device_id=(dev,), device_id_type=MESH
        )

    row8 = lax.broadcasted_iota(jnp.int32, (8, PTS), 0)

    barrier = pltpu.get_barrier_semaphore()

    def greet(dev):
        pl.semaphore_signal(barrier, inc=1, device_id=(dev,), device_id_type=MESH)

    greet(partner)
    for i in range(1, NG):
        greet(peer_a(i))
        greet(peer_b(i))

    z_near = (1, 2, NZ - 2, NZ - 1) if NZ == 16 else tuple(range(1, NZ))
    for i in z_near:
        greet(peer_z(i))
    n_greet = 1 + 2 * (NG - 1) + len(z_near)

    def tell(sem, reach):
        if NZ == 16:
            for i in (reach, NZ - reach):
                pl.semaphore_signal(sem, inc=1, device_id=(peer_z(i),), device_id_type=MESH)

    def step_near():
        if NZ == 16:
            pl.semaphore_wait(near_s, 2)
        tell(far_s, 4)

    def step_far():
        if NZ == 16:
            pl.semaphore_wait(far_s, 2)

    @pl.when(me > 0)
    def _():
        greet(me - 1)

    @pl.when(me < count - 1)
    def _():
        greet(me + 1)

    def load(i):
        src = (dens_in, pts_in, ch_in, surf_in, up_in, low_in, upp_in, down_in)[i]
        dst = (dens, pts, ch, surf, maps.at[0], maps.at[1], maps.at[2], maps.at[3])[i]
        return pltpu.make_async_copy(src, dst, load_s.at[i])

    for i in range(8):
        load(i).start()

    mine = a * 2 + core
    lane = lax.broadcasted_iota(jnp.int32, (8, SP), 1) % ROWS
    tail_q = lax.broadcasted_iota(jnp.int32, (Q, SP - S), 0)
    keys = jnp.zeros((8, SP), jnp.int32)
    for l in range(LB):
        keys = jnp.where(lane // Q == l, octs[l], keys)
    rbuf[mine, ROWS : ROWS + 8, :] = (keys * Q + lane % Q).astype(F32)
    load(0).wait()
    for l in range(LB):
        rbuf[mine, Q * l : Q * l + Q, 0:S] = dens[l]
        rbuf[mine, Q * l : Q * l + Q, S:SP] = (tail_q + octs[l] * Q).astype(F32)

    n_wait = n_greet + (me + count - 1) // count + (2 * count - 2 - me) // count
    pl.semaphore_wait(barrier, n_wait)

    def halo(i):
        dev = me + 1 - 2 * i
        return (
            send(pts_in, hp.at[i], halo_s.at[i], halo_r.at[i], dev),
            send(ch_in, hc.at[i], halo_s.at[2 + i], halo_r.at[2 + i], dev),
        )

    core_out = send(rbuf.at[mine], rbuf.at[a_partner * 2 + core], core_s, core_r, partner)
    core_in = send(rbuf.at[mine], rbuf.at[a * 2 + 1 - core], core_s, core_r, partner)

    def row_copy(s, r, i, slot):
        return send(rbuf.at[slot], rbuf.at[slot], s.at[i], r.at[i], peer_a(i))

    def am_copy(i, at):
        return row_copy(am_s, am_r, i, at * 2 + core)

    def ao_copy(i, at):
        return row_copy(ao_s, ao_r, i, at * 2 + 1 - core)

    def b_copy(i, chunk, at):
        return send(p1.at[pl.ds(chunk * NZ * Q, NZ * Q)], qb.at[at], b_s.at[i], b_r.at[i], peer_b(i))

    def z_copy(i, chunk, at):
        return send(p2.at[chunk], zb.at[at], z_s.at[i], z_r.at[i], peer_z(i))

    def gz_copy(i, at):
        return send(gz.at[at], gz.at[at], gz_s.at[i], gz_r.at[i], peer_z(i))

    def gb_copy(i, at):
        return send(wb.at[at], wb.at[at], gb_s.at[i], gb_r.at[i], peer_b(i))

    def v_copy(i, chunk, at):
        return send(sbuf.at[pl.ds(chunk * 2, 2)], vbuf.at[at], v_s.at[i], v_r.at[i], peer_a(i))

    core_out.start()
    for i in range(1, NG):
        am_copy(i, a).start()
    tell(near_s, 2)

    @pl.when(me < count - 1)
    def _():
        for c in halo(0):
            c.start()

    @pl.when(me > 0)
    def _():
        for c in halo(1):
            c.start()

    def step_a():
        core_in.wait_recv()
        for i in range(1, NG):
            ao_copy(i, a).start()

    def step_b():
        for i in range(1, NG):
            am_copy(i, (a + NG - i) % NG).wait_recv()
            ao_copy(i, (a + NG - i) % NG).wait_recv()
        rows = lax.broadcasted_iota(jnp.int32, (NG * NZ * Q, 3 * ROWS), 0) + oct_a * Q
        rows = rows.astype(F32)

        def add(j, _):
            member = jnp.where(rows == rbuf[j, ROWS : ROWS + 1, 0 : 3 * ROWS], 1.0, 0.0).astype(BF16)
            parts = jnp.concatenate(split3(rbuf[j, 0:ROWS, :]), axis=0).astype(BF16)
            p1[...] += jnp.dot(member, parts, preferred_element_type=F32)
            return 0

        p1[...] = jnp.zeros(p1.shape, F32)
        lax.fori_loop(0, 2 * NG, add, 0)
        for i in range(1, NG):
            b_copy(i, (b + i) % NG, b).start()

    def step_z():
        total = p1[pl.ds(pl.multiple_of(b * NZ * Q, 8), NZ * Q), :]
        for i in range(1, NG):
            at = (b + NG - i) % NG
            b_copy(i, at, at).wait_recv()
            total = total + qb[at]
        for j in range(NZ):
            p2[j] = total[Q * j : Q * j + Q, :]

        def go(i, _):
            z_copy(i, (z + i) % NZ, z).start()
            return 0

        lax.fori_loop(1, NZ, go, 0)

    def step_gz():
        def take(i, total):
            at = (z + NZ - i) % NZ
            z_copy(i, at, at).wait_recv()
            return total + zb[at]

        gz[z] = lax.fori_loop(1, NZ, take, p2[z])

        def go(i, _):
            gz_copy(i, z).start()
            return 0

        lax.fori_loop(1, NZ, go, 0)

    def step_gb():
        def take(i, _):
            gz_copy(i, (z + NZ - i) % NZ).wait_recv()
            return 0

        lax.fori_loop(1, NZ, take, 0)
        for j in range(NZ):
            g2[Q * j : Q * j + Q, :] = gz[j]
        e = dot3(g2[:, 0:S], maps_hi[0], maps_lo[0])
        none = jnp.zeros((8, S), F32)
        w = jnp.concatenate([none, dot3(e, maps_hi[1], maps_lo[1])], axis=0) + jnp.concatenate(
            [dot3(e, maps_hi[2], maps_lo[2]), none], axis=0
        )
        wb[b] = jnp.zeros(wb.shape[1:], F32)
        wb[b, :, 0:S] = dot3(w, maps_hi[3], maps_lo[3]) * INV_FOUR_PI
        for i in range(1, NG):
            gb_copy(i, b).start()

    def step_v():
        for i in range(1, NG):
            gb_copy(i, (b + NG - i) % NG).wait_recv()
        ext = NZ * Q + 8
        cols = lax.broadcasted_iota(jnp.int32, (2 * ROWS, NG * ext), 1)
        cols = cols % ext + (cols // ext) * (NZ * Q) + (oct_a - 1) * Q
        cols = cols.astype(F32)
        hi, lo = split2(wb[...].reshape(NG * ext, SP))
        for i in list(range(1, NG)) + [0]:
            at = (a + i) % NG
            key = rbuf[pl.ds(at * 2, 2), 0:ROWS, S : S + 1].reshape(2 * ROWS, 1)
            member = jnp.where(cols == key, 1.0, 0.0).astype(BF16)
            picked = jnp.dot(member, hi, preferred_element_type=F32) + jnp.dot(
                member, lo, preferred_element_type=F32
            )
            sbuf[pl.ds(at * 2, 2)] = picked.reshape(2, ROWS, SP)
            if i > 0:
                v_copy(i, at, a).start()

    def e_copy(c):
        return send(tot.at[c], ebuf, e_s, e_r, partner)

    def step_e():
        total = sbuf[pl.ds(a * 2, 2)]
        for i in range(1, NG):
            at = (a + NG - i) % NG
            v_copy(i, at, at).wait_recv()
            total = total + vbuf[at]
        tot[...] = total
        e_copy(1 - core).start()

    steps = (step_a, step_near, step_far, step_b, step_z, step_gz, step_gb, step_v, step_e)

    def run_steps(at):
        for place, step in zip(STEP_AT, steps):

            @pl.when(at == place)
            def _():
                step()

    def prep(n, p, q):
        fs[n] = source_features(p, row8).T.astype(BF16)
        hi = q.astype(BF16).astype(F32)
        lo = q - hi
        cw[n] = jnp.concatenate([hi + pltpu.roll(lo, 4, 0), jnp.zeros((8, PTS), F32)], axis=0).astype(BF16)

    xp[...] = jnp.zeros(xp.shape, F32)
    load(1).wait()
    load(2).wait()

    def prep_own(n, _):
        for c in range(3):
            xp[n, c : c + 1, :] = pts[c, pl.ds(n, 1), :]
        xp[LB, 0:4, :] = ch[n] * INV_FOUR_PI
        prep(n, xp[n], xp[LB])
        return 0

    lax.fori_loop(0, LB, prep_own, 0)
    for i in range(3, 8):
        load(i).wait()
    fsurf[...] = surf[...].astype(BF16)
    for i in range(4):
        maps_hi[i], maps_lo[i] = split2(maps[i])

    def own_pair(t, _):
        for h in range(2):
            l = 2 * t + h
            near[l] = pair_sum(fs[l], target_features(xp[l], row8), cw[l])
        run_steps(2 * t)
        return 0

    lax.fori_loop(0, LB // 2, own_pair, 0)

    for i in range(2):
        present = me > 0 if i == 0 else me < count - 1

        @pl.when(present)
        def _():
            for c in halo(i):
                c.wait_recv()

        @pl.when(jnp.logical_not(present))
        def _():
            hp[i] = jnp.zeros(hp.shape[1:], F32)
            hc[i] = jnp.zeros(hc.shape[1:], F32)

    for i in range(2):

        def prep_halo(j, _):
            n = users[i, j]
            for c in range(3):
                xp[LB + 1, c : c + 1, :] = hp[i, c, pl.ds(n, 1), :]
            xp[LB, 0:4, :] = hc[i, n] * INV_FOUR_PI
            prep(LB + i * UH + j, xp[LB + 1], xp[LB])
            return 0

        lax.fori_loop(0, UH, prep_halo, 0)

    def near_leaf(l, _):
        acc = near[l]
        box = xp[l]
        for k in range(K):
            n = nears[k, l]
            code = codes[k, l]
            code = jnp.where(code >= 13, code + 1, code)
            ox = (2 * (code // 9 - 1)).astype(F32)
            oy = (2 * ((code // 3) % 3 - 1)).astype(F32)
            oz = (2 * (code % 3 - 1)).astype(F32)
            off = jnp.where(row8 == 0, ox, jnp.where(row8 == 1, oy, jnp.where(row8 == 2, oz, 0.0)))
            acc = acc + pair_sum(fs[n], target_features(box - off, row8), cw[n])
        near[l] = acc
        run_steps(LB + l)
        return 0

    lax.fori_loop(0, LB, near_leaf, 0)

    def far_leaf(l, _):
        gh[l], gl[l] = green(fsurf[...], target_features(xp[l], row8))
        run_steps(2 * LB + l)
        return 0

    lax.fori_loop(0, LB, far_leaf, 0)

    e_copy(core).wait_recv()
    w = tot[core] + ebuf[...]
    hi = w.astype(BF16).astype(F32)
    lo = w - hi
    for t in range(LB // 2):
        pair = jnp.concatenate([hi[8 * t : 8 * t + 8], lo[8 * t : 8 * t + 8]], axis=0)
        cfar[t] = pair.astype(BF16)

    def far_pair(t, _):
        for h in range(2):
            l = 2 * t + h
            c = cfar[t, :, 0:FAR]
            far = jnp.dot(c, gh[l], preferred_element_type=F32) + jnp.dot(
                c, gl[l], preferred_element_type=F32
            )
            far = far[0:8] + far[8:16]
            out[l] = far[4 * h : 4 * h + 4] + near[l, 0:4, :] + near[l, 4:8, :]
        return 0

    lax.fori_loop(0, LB // 2, far_pair, 0)

    core_out.wait_send()

    @pl.when(me < count - 1)
    def _():
        for c in halo(0):
            c.wait_send()

    @pl.when(me > 0)
    def _():
        for c in halo(1):
            c.wait_send()

    for i in range(1, NG):
        am_copy(i, a).wait_send()
        ao_copy(i, a).wait_send()
        b_copy(i, (b + i) % NG, b).wait_send()
        gb_copy(i, b).wait_send()
        v_copy(i, (a + i) % NG, a).wait_send()

    def sent_z(i, _):
        z_copy(i, (z + i) % NZ, z).wait_send()
        gz_copy(i, z).wait_send()
        return 0

    lax.fori_loop(1, NZ, sent_z, 0)
    e_copy(1 - core).wait_send()


STEP_AT = (0, 6, 12, 8, 14, 19, 23, 27, 32)


def body(points, charges, leaf_density, leaf_octant, user_lists, near_leaves, near_codes,
         upward_map, lower_map, upper_map, downward_map):
    smem = pl.BlockSpec(memory_space=pltpu.SMEM)
    hbm = pl.BlockSpec(memory_space=pltpu.HBM)
    dma = pltpu.SemaphoreType.DMA
    return pl.pallas_call(
        kernel,
        out_shape=jax.ShapeDtypeStruct((LB, Q, PTS), F32),
        in_specs=[smem] * 4 + [hbm] * 8,
        out_specs=pl.BlockSpec(memory_space=pltpu.VMEM),
        scratch_shapes=[
            pltpu.VMEM((3, LB, PTS), F32),
            pltpu.VMEM((LB, Q, PTS), F32),
            pltpu.VMEM((LB, Q, S), F32),
            pltpu.VMEM((4, S, S), F32),
            pltpu.VMEM((FAR, 48), F32),
            pltpu.VMEM((4, S, S), BF16),
            pltpu.VMEM((4, S, S), BF16),
            pltpu.VMEM((FAR, 48), BF16),
            pltpu.VMEM((LB + 2, 8, PTS), F32),
            pltpu.VMEM((LB + 2 * UH, PTS, 48), BF16),
            pltpu.VMEM((LB + 2 * UH, 16, PTS), BF16),
            pltpu.VMEM((2, 3, LB, PTS), F32),
            pltpu.VMEM((2, LB, Q, PTS), F32),
            pltpu.VMEM((LB, 16, PTS), F32),
            pltpu.VMEM((2 * NG, ROWS + 8, SP), F32),
            pltpu.VMEM((NG * NZ * Q, SP), F32),
            pltpu.VMEM((NG, NZ * Q, SP), F32),
            pltpu.VMEM((NZ, Q, SP), F32),
            pltpu.VMEM((NZ, Q, SP), F32),
            pltpu.VMEM((NZ, Q, SP), F32),
            pltpu.VMEM((NZ * Q, SP), F32),
            pltpu.VMEM((NG, NZ * Q + 8, SP), F32),
            pltpu.VMEM((2 * NG, ROWS, SP), F32),
            pltpu.VMEM((NG, 2, ROWS, SP), F32),
            pltpu.VMEM((2, ROWS, SP), F32),
            pltpu.VMEM((ROWS, SP), F32),
            pltpu.VMEM((LB // 2, 16, SP), BF16),
            pltpu.VMEM((LB, FAR, PTS), BF16),
            pltpu.VMEM((LB, FAR, PTS), BF16),
            pltpu.SemaphoreType.REGULAR, pltpu.SemaphoreType.REGULAR,
            dma((8,)), dma((4,)), dma((4,)), dma, dma,
            dma((NG,)), dma((NG,)), dma((NG,)), dma((NG,)),
            dma((NG,)), dma((NG,)), dma((NZ,)), dma((NZ,)), dma((NZ,)), dma((NZ,)),
            dma((NG,)), dma((NG,)), dma((NG,)), dma((NG,)), dma, dma,
        ],
        compiler_params=pltpu.CompilerParams(
            collective_id=0, has_side_effects=True, vmem_limit_bytes=56 * 2**20
        ),
    )(
        leaf_octant, user_lists.reshape(2, UH), near_leaves.T, near_codes.T,
        points.transpose(1, 0, 2), charges, leaf_density,
        upward_map, lower_map, upper_map, downward_map, jnp.asarray(surface_features(), F32),
    )


def solution(mesh):
    in_specs = (
        P("cube", None, None),
        P("cube", None, None),
        P("cube", None, None),
        P("cube"),
        P("cube", None, None),
        P("cube", None),
        P("cube", None),
        P(),
        P(),
        P(),
        P(),
    )
    return jax.shard_map(
        body, mesh=mesh, in_specs=in_specs, out_specs=P("cube", None, None), check_vma=False
    )
```

```python
import functools
import math

import jax
import jax.numpy as jnp
import numpy as np
from jax import lax
from jax.experimental import pallas as pl
from jax.experimental.pallas import tpu as pltpu
from jax.sharding import PartitionSpec as P

EQ_ORDER = 8
INV_FOUR_PI = 1.0 / (4.0 * math.pi)
SOFTEN = 0.01
LB = 16
UH = 4
K = 4
Q = 4
S = 296
SP = 384
PTS = 512
FAR = 304
ROWS = LB * Q
MESH = pl.DeviceIdType.MESH
F32 = jnp.float32
BF16 = jnp.bfloat16
NX, NY, NZ = 4, 4, 16
NG = 4


def surface_table():
    spacing = np.linspace(-1.0, 1.0, EQ_ORDER)
    mesh_x, mesh_y, mesh_z = np.meshgrid(spacing, spacing, spacing, indexing="ij")
    lattice = np.stack([mesh_x.ravel(), mesh_y.ravel(), mesh_z.ravel()], 0)
    on_boundary = np.max(np.abs(lattice), axis=0) > 0.999
    return lattice[:, on_boundary] * 2.95


def split3(v):
    a = v.astype(BF16).astype(F32)
    r = v - a
    b = r.astype(BF16).astype(F32)
    return a, b, r - b


def source_features(p, row):
    nsq = jnp.sum(p * p, axis=0, keepdims=True)
    u = jnp.where(row == 3, nsq, jnp.where(row == 4, 1.0, p))
    a, b, c = split3(u)
    return jnp.concatenate([a, a, b, b, a, c], axis=0)


def target_features(t, row):
    nsq = jnp.sum(t * t, axis=0, keepdims=True) + SOFTEN
    v = jnp.where(row == 3, 1.0, jnp.where(row == 4, nsq, -2.0 * t))
    a, b, c = split3(v)
    return jnp.concatenate([a, b, a, b, c, a], axis=0).astype(BF16)


def surface_features():
    pts = np.zeros((8, FAR), np.float32)
    pts[:3, :S] = surface_table().astype(np.float32)
    pts[:3, S:] = pts[:3, :1]
    u = pts.copy()
    u[3] = np.sum(pts * pts, axis=0)
    u[4] = 1.0
    a = u.astype(jnp.bfloat16).astype(np.float32)
    b = (u - a).astype(jnp.bfloat16).astype(np.float32)
    c = u - a - b
    return np.ascontiguousarray(np.concatenate([a, a, b, b, a, c], axis=0).T)


def green(feat, ft):
    g = lax.rsqrt(jnp.dot(feat, ft, preferred_element_type=F32))
    hi = g.astype(BF16)
    return hi, (g - hi.astype(F32)).astype(BF16)


def pair_sum(feat, ft, weights):
    parts = []
    for at in range(0, PTS, 256):
        hi, lo = green(feat, ft[:, at : at + 256])
        parts.append(
            jnp.dot(weights, hi, preferred_element_type=F32)
            + jnp.dot(weights, lo, preferred_element_type=F32)
        )
    return jnp.concatenate(parts, axis=1)


def split2(v):
    hi = v.astype(BF16)
    return hi, (v - hi.astype(F32)).astype(BF16)


def dot3(x, w_hi, w_lo):
    hi, lo = split2(x)
    n = x.shape[0]
    both = jnp.concatenate([hi, lo], axis=0)
    r = jnp.dot(both, w_hi, preferred_element_type=F32)
    return r[:n] + r[n:] + jnp.dot(hi, w_lo, preferred_element_type=F32)


def kernel(
    octs, users, nears, codes, pts_in, ch_in, dens_in, up_in, low_in, upp_in, down_in, surf_in,
    out,
    pts, ch, dens, maps, surf, maps_hi, maps_lo, fsurf,
    xp, fs, cw, hp, hc, near, rbuf, p1, qb, p2, zb, gz, g2, wb, sbuf, vbuf, cfar, gh, gl,
    near_s, far_s, load_s, halo_s, halo_r, a_s, a_r, b_s, b_r, z_s, z_r,
    gz_s, gz_r, gb_s, gb_r, v_s, v_r,
):
    me = lax.axis_index("cube")
    count = 2 * NX * NY * NZ
    core = me % 2
    z = (me // 2) % NZ
    y = (me // (2 * NZ)) % NY
    x = me // (2 * NZ * NY)
    stride_x, stride_y = 2 * NZ * NY, 2 * NZ
    stride_a = stride_x * (1 - core) + stride_y * core
    stride_b = stride_y * (1 - core) + stride_x * core
    a = x * (1 - core) + y * core
    b = y * (1 - core) + x * core
    partner = me + 1 - 2 * core
    oct_a = core * (NG * NG * NZ) + a * (NG * NZ)

    def peer_a(i):
        return me + ((a + i) % NG - a) * stride_a

    def peer_b(i):
        return me + ((b + i) % NG - b) * stride_b

    def peer_z(i):
        return me + ((z + i) % NZ - z) * 2

    def cross_a(i):
        return peer_a(i) + 1 - 2 * core

    def cross_b(i):
        return peer_b(i) + 1 - 2 * core

    def far_first(t):
        return NZ // 2 + (t + 1) // 2 * (1 - 2 * (t % 2))

    def send(src, dst, s, r, dev):
        return pltpu.make_async_remote_copy(
            src_ref=src, dst_ref=dst, send_sem=s, recv_sem=r, device_id=(dev,), device_id_type=MESH
        )

    row8 = lax.broadcasted_iota(jnp.int32, (8, PTS), 0)

    barrier = pltpu.get_barrier_semaphore()

    def greet(dev):
        pl.semaphore_signal(barrier, inc=1, device_id=(dev,), device_id_type=MESH)

    greet(partner)
    for i in range(1, NG):
        greet(peer_a(i))
        greet(peer_b(i))
        greet(cross_a(i))
        greet(cross_b(i))

    z_near = (1, 2, NZ - 2, NZ - 1) if NZ == 16 else tuple(range(1, NZ))
    for i in z_near:
        greet(peer_z(i))
    n_greet = 1 + 4 * (NG - 1) + len(z_near)

    def tell(sem, reach):
        if NZ == 16:
            for i in (reach, NZ - reach):
                pl.semaphore_signal(sem, inc=1, device_id=(peer_z(i),), device_id_type=MESH)

    def step_near():
        if NZ == 16:
            pl.semaphore_wait(near_s, 2)
        tell(far_s, 4)

    def step_far():
        if NZ == 16:
            pl.semaphore_wait(far_s, 2)

    @pl.when(me > 0)
    def _():
        greet(me - 1)

    @pl.when(me < count - 1)
    def _():
        greet(me + 1)

    def load(i):
        src = (dens_in, pts_in, ch_in, surf_in, up_in, low_in, upp_in, down_in)[i]
        dst = (dens, pts, ch, surf, maps.at[0], maps.at[1], maps.at[2], maps.at[3])[i]
        return pltpu.make_async_copy(src, dst, load_s.at[i])

    for i in range(8):
        load(i).start()

    mine = a * 2 + core
    lane = lax.broadcasted_iota(jnp.int32, (8, SP), 1) % ROWS
    tail_q = lax.broadcasted_iota(jnp.int32, (Q, SP - S), 0)
    keys = jnp.zeros((8, SP), jnp.int32)
    for l in range(LB):
        keys = jnp.where(lane // Q == l, octs[l], keys)
    rbuf[mine, ROWS : ROWS + 8, :] = (keys * Q + lane % Q).astype(F32)
    load(0).wait()
    for l in range(LB):
        rbuf[mine, Q * l : Q * l + Q, 0:S] = dens[l]
        rbuf[mine, Q * l : Q * l + Q, S:SP] = (tail_q + octs[l] * Q).astype(F32)

    n_wait = n_greet + (me + count - 1) // count + (2 * count - 2 - me) // count
    pl.semaphore_wait(barrier, n_wait)

    def halo(i):
        dev = me + 1 - 2 * i
        return (
            send(pts_in, hp.at[i], halo_s.at[i], halo_r.at[i], dev),
            send(ch_in, hc.at[i], halo_s.at[2 + i], halo_r.at[2 + i], dev),
        )

    def a_copy(i, slot):
        dev = peer_a(i) if i < NG else cross_b(i - NG)
        return send(rbuf.at[mine], rbuf.at[slot], a_s.at[i], a_r.at[i], dev)

    def a_send(i):
        return a_copy(i, mine if i < NG else b * 2 + core)

    def a_take(i):
        return a_copy(i, (a + 2 * NG - i) % NG * 2 + (core if i < NG else 1 - core))

    a_all = tuple(range(1, 2 * NG))

    def b_copy(i, chunk, at):
        return send(p1.at[pl.ds(chunk * NZ * Q, NZ * Q)], qb.at[at], b_s.at[i], b_r.at[i], peer_b(i))

    def z_copy(i, chunk, at):
        return send(p2.at[chunk], zb.at[at], z_s.at[i], z_r.at[i], peer_z(i))

    def gz_copy(i, at):
        return send(gz.at[at], gz.at[at], gz_s.at[i], gz_r.at[i], peer_z(i))

    def gb_copy(i, at):
        return send(wb.at[at], wb.at[at], gb_s.at[i], gb_r.at[i], peer_b(i))

    def v_copy(i, at):
        dev = peer_a(i) if i < NG else cross_a(i - NG)
        slot = (a + i) % NG * 2 + (core if i < NG else 1 - core)
        return send(sbuf.at[slot], vbuf.at[at], v_s.at[i], v_r.at[i], dev)

    def v_send(i):
        return v_copy(i, a if i < NG else NG + a)

    def v_place(i):
        return (a + NG - i) % NG if i < NG else NG + (b + 2 * NG - i) % NG

    for i in a_all:
        a_send(i).start()
    tell(near_s, 2)

    @pl.when(me < count - 1)
    def _():
        for c in halo(0):
            c.start()

    @pl.when(me > 0)
    def _():
        for c in halo(1):
            c.start()

    def step_b():
        for i in a_all:
            a_take(i).wait_recv()
        rows = lax.broadcasted_iota(jnp.int32, (NG * NZ * Q, 3 * ROWS), 0) + oct_a * Q
        rows = rows.astype(F32)

        def add(j, _):
            member = jnp.where(rows == rbuf[j, ROWS : ROWS + 1, 0 : 3 * ROWS], 1.0, 0.0).astype(BF16)
            parts = jnp.concatenate(split3(rbuf[j, 0:ROWS, :]), axis=0).astype(BF16)
            p1[...] += jnp.dot(member, parts, preferred_element_type=F32)
            return 0

        p1[...] = jnp.zeros(p1.shape, F32)
        lax.fori_loop(0, 2 * NG, add, 0)
        for i in range(1, NG):
            b_copy(i, (b + i) % NG, b).start()

    def step_z():
        total = p1[pl.ds(pl.multiple_of(b * NZ * Q, 8), NZ * Q), :]
        for i in range(1, NG):
            at = (b + NG - i) % NG
            b_copy(i, at, at).wait_recv()
            total = total + qb[at]
        for j in range(NZ):
            p2[j] = total[Q * j : Q * j + Q, :]

        def go(t, _):
            i = far_first(t)
            z_copy(i, (z + i) % NZ, z).start()
            return 0

        lax.fori_loop(0, NZ - 1, go, 0)

    def step_gz():
        def take(i, total):
            at = (z + NZ - i) % NZ
            z_copy(i, at, at).wait_recv()
            return total + zb[at]

        gz[z] = lax.fori_loop(1, NZ, take, p2[z])

        def go(t, _):
            gz_copy(far_first(t), z).start()
            return 0

        lax.fori_loop(0, NZ - 1, go, 0)

    def step_gb():
        def take(i, _):
            gz_copy(i, (z + NZ - i) % NZ).wait_recv()
            return 0

        lax.fori_loop(1, NZ, take, 0)
        for j in range(NZ):
            g2[Q * j : Q * j + Q, :] = gz[j]
        e = dot3(g2[:, 0:S], maps_hi[0], maps_lo[0])
        none = jnp.zeros((8, S), F32)
        w = jnp.concatenate([none, dot3(e, maps_hi[1], maps_lo[1])], axis=0) + jnp.concatenate(
            [dot3(e, maps_hi[2], maps_lo[2]), none], axis=0
        )
        wb[b] = jnp.zeros(wb.shape[1:], F32)
        wb[b, :, 0:S] = dot3(w, maps_hi[3], maps_lo[3]) * INV_FOUR_PI
        for i in range(1, NG):
            gb_copy(i, b).start()

    def step_v():
        for i in range(1, NG):
            gb_copy(i, (b + NG - i) % NG).wait_recv()
        ext = NZ * Q + 8
        cols = lax.broadcasted_iota(jnp.int32, (2 * ROWS, NG * ext), 1)
        cols = cols % ext + (cols // ext) * (NZ * Q) + (oct_a - 1) * Q
        cols = cols.astype(F32)
        hi, lo = split2(wb[...].reshape(NG * ext, SP))
        for i in list(range(1, NG)) + [0]:
            at = (a + i) % NG
            key = rbuf[pl.ds(at * 2, 2), 0:ROWS, S : S + 1].reshape(2 * ROWS, 1)
            member = jnp.where(cols == key, 1.0, 0.0).astype(BF16)
            picked = jnp.dot(member, hi, preferred_element_type=F32) + jnp.dot(
                member, lo, preferred_element_type=F32
            )
            sbuf[pl.ds(at * 2, 2)] = picked.reshape(2, ROWS, SP)
            if i > 0:
                v_send(i).start()
            v_send(NG + i).start()

    steps = (step_near, step_far, step_b, step_z, step_gz, step_gb, step_v)

    def run_steps(at):
        for place, step in zip(STEP_AT, steps):

            @pl.when(at == place)
            def _():
                step()

    def prep(n, p, q):
        fs[n] = source_features(p, row8).T.astype(BF16)
        hi = q.astype(BF16).astype(F32)
        lo = q - hi
        cw[n] = jnp.concatenate([hi + pltpu.roll(lo, 4, 0), jnp.zeros((8, PTS), F32)], axis=0).astype(BF16)

    xp[...] = jnp.zeros(xp.shape, F32)
    load(1).wait()
    load(2).wait()

    def prep_own(n, _):
        for c in range(3):
            xp[n, c : c + 1, :] = pts[c, pl.ds(n, 1), :]
        xp[LB, 0:4, :] = ch[n] * INV_FOUR_PI
        prep(n, xp[n], xp[LB])
        return 0

    lax.fori_loop(0, LB, prep_own, 0)
    for i in range(3, 8):
        load(i).wait()
    fsurf[...] = surf[...].astype(BF16)
    for i in range(4):
        maps_hi[i], maps_lo[i] = split2(maps[i])

    def own_pair(t, _):
        for h in range(2):
            l = 2 * t + h
            near[l] = pair_sum(fs[l], target_features(xp[l], row8), cw[l])
        run_steps(2 * t)
        return 0

    lax.fori_loop(0, LB // 2, own_pair, 0)

    for i in range(2):
        present = me > 0 if i == 0 else me < count - 1

        @pl.when(present)
        def _():
            for c in halo(i):
                c.wait_recv()

        @pl.when(jnp.logical_not(present))
        def _():
            hp[i] = jnp.zeros(hp.shape[1:], F32)
            hc[i] = jnp.zeros(hc.shape[1:], F32)

    for i in range(2):

        def prep_halo(j, _):
            n = users[i, j]
            for c in range(3):
                xp[LB + 1, c : c + 1, :] = hp[i, c, pl.ds(n, 1), :]
            xp[LB, 0:4, :] = hc[i, n] * INV_FOUR_PI
            prep(LB + i * UH + j, xp[LB + 1], xp[LB])
            return 0

        lax.fori_loop(0, UH, prep_halo, 0)

    def near_leaf(l, _):
        acc = near[l]
        box = xp[l]
        for k in range(K):
            n = nears[k, l]
            code = codes[k, l]
            code = jnp.where(code >= 13, code + 1, code)
            ox = (2 * (code // 9 - 1)).astype(F32)
            oy = (2 * ((code // 3) % 3 - 1)).astype(F32)
            oz = (2 * (code % 3 - 1)).astype(F32)
            off = jnp.where(row8 == 0, ox, jnp.where(row8 == 1, oy, jnp.where(row8 == 2, oz, 0.0)))
            acc = acc + pair_sum(fs[n], target_features(box - off, row8), cw[n])
        near[l] = acc
        run_steps(LB + l)
        return 0

    lax.fori_loop(0, LB, near_leaf, 0)

    def far_leaf(l, _):
        gh[l], gl[l] = green(fsurf[...], target_features(xp[l], row8))
        run_steps(2 * LB + l)
        return 0

    lax.fori_loop(0, LB, far_leaf, 0)

    w = sbuf[mine]
    for i in a_all:
        v_copy(i, v_place(i)).wait_recv()
        w = w + vbuf[v_place(i)]
    hi = w.astype(BF16).astype(F32)
    lo = w - hi
    for t in range(LB // 2):
        pair = jnp.concatenate([hi[8 * t : 8 * t + 8], lo[8 * t : 8 * t + 8]], axis=0)
        cfar[t] = pair.astype(BF16)

    def far_pair(t, _):
        for h in range(2):
            l = 2 * t + h
            c = cfar[t, :, 0:FAR]
            far = jnp.dot(c, gh[l], preferred_element_type=F32) + jnp.dot(
                c, gl[l], preferred_element_type=F32
            )
            far = far[0:8] + far[8:16]
            out[l] = far[4 * h : 4 * h + 4] + near[l, 0:4, :] + near[l, 4:8, :]
        return 0

    lax.fori_loop(0, LB // 2, far_pair, 0)

    for i in a_all:
        a_send(i).wait_send()
        v_send(i).wait_send()

    @pl.when(me < count - 1)
    def _():
        for c in halo(0):
            c.wait_send()

    @pl.when(me > 0)
    def _():
        for c in halo(1):
            c.wait_send()

    for i in range(1, NG):
        b_copy(i, (b + i) % NG, b).wait_send()
        gb_copy(i, b).wait_send()

    def sent_z(i, _):
        z_copy(i, (z + i) % NZ, z).wait_send()
        gz_copy(i, z).wait_send()
        return 0

    lax.fori_loop(1, NZ, sent_z, 0)


STEP_AT = (0, 6, 14, 17, 23, 28, 36)


def body(points, charges, leaf_density, leaf_octant, user_lists, near_leaves, near_codes,
         upward_map, lower_map, upper_map, downward_map):
    smem = pl.BlockSpec(memory_space=pltpu.SMEM)
    hbm = pl.BlockSpec(memory_space=pltpu.HBM)
    dma = pltpu.SemaphoreType.DMA
    return pl.pallas_call(
        kernel,
        out_shape=jax.ShapeDtypeStruct((LB, Q, PTS), F32),
        in_specs=[smem] * 4 + [hbm] * 8,
        out_specs=pl.BlockSpec(memory_space=pltpu.VMEM),
        scratch_shapes=[
            pltpu.VMEM((3, LB, PTS), F32),
            pltpu.VMEM((LB, Q, PTS), F32),
            pltpu.VMEM((LB, Q, S), F32),
            pltpu.VMEM((4, S, S), F32),
            pltpu.VMEM((FAR, 48), F32),
            pltpu.VMEM((4, S, S), BF16),
            pltpu.VMEM((4, S, S), BF16),
            pltpu.VMEM((FAR, 48), BF16),
            pltpu.VMEM((LB + 2, 8, PTS), F32),
            pltpu.VMEM((LB + 2 * UH, PTS, 48), BF16),
            pltpu.VMEM((LB + 2 * UH, 16, PTS), BF16),
            pltpu.VMEM((2, 3, LB, PTS), F32),
            pltpu.VMEM((2, LB, Q, PTS), F32),
            pltpu.VMEM((LB, 16, PTS), F32),
            pltpu.VMEM((2 * NG, ROWS + 8, SP), F32),
            pltpu.VMEM((NG * NZ * Q, SP), F32),
            pltpu.VMEM((NG, NZ * Q, SP), F32),
            pltpu.VMEM((NZ, Q, SP), F32),
            pltpu.VMEM((NZ, Q, SP), F32),
            pltpu.VMEM((NZ, Q, SP), F32),
            pltpu.VMEM((NZ * Q, SP), F32),
            pltpu.VMEM((NG, NZ * Q + 8, SP), F32),
            pltpu.VMEM((2 * NG, ROWS, SP), F32),
            pltpu.VMEM((2 * NG, ROWS, SP), F32),
            pltpu.VMEM((LB // 2, 16, SP), BF16),
            pltpu.VMEM((LB, FAR, PTS), BF16),
            pltpu.VMEM((LB, FAR, PTS), BF16),
            pltpu.SemaphoreType.REGULAR, pltpu.SemaphoreType.REGULAR,
            dma((8,)), dma((4,)), dma((4,)), dma((2 * NG,)), dma((2 * NG,)),
            dma((NG,)), dma((NG,)), dma((NZ,)), dma((NZ,)), dma((NZ,)), dma((NZ,)),
            dma((NG,)), dma((NG,)), dma((2 * NG,)), dma((2 * NG,)),
        ],
        compiler_params=pltpu.CompilerParams(
            collective_id=0, has_side_effects=True, vmem_limit_bytes=56 * 2**20
        ),
    )(
        leaf_octant, user_lists.reshape(2, UH), near_leaves.T, near_codes.T,
        points.transpose(1, 0, 2), charges, leaf_density,
        upward_map, lower_map, upper_map, downward_map, jnp.asarray(surface_features(), F32),
    )


def solution(mesh):
    in_specs = (
        P("cube", None, None),
        P("cube", None, None),
        P("cube", None, None),
        P("cube"),
        P("cube", None, None),
        P("cube", None),
        P("cube", None),
        P(),
        P(),
        P(),
        P(),
    )
    return jax.shard_map(
        body, mesh=mesh, in_specs=in_specs, out_specs=P("cube", None, None), check_vma=False
    )
```

```python
import functools
import math

import jax
import jax.numpy as jnp
import numpy as np
from jax import lax
from jax.experimental import pallas as pl
from jax.experimental.pallas import tpu as pltpu
from jax.sharding import PartitionSpec as P

EQ_ORDER = 8
INV_FOUR_PI = 1.0 / (4.0 * math.pi)
SOFTEN = 0.01
LB = 16
UH = 4
K = 4
Q = 4
S = 296
SP = 384
PTS = 512
FAR = 304
ROWS = LB * Q
TAIL = S - 256
PACKED = 2 * ROWS + 24
MESH = pl.DeviceIdType.MESH
F32 = jnp.float32
BF16 = jnp.bfloat16
NX, NY, NZ = 4, 4, 16
NG = 4


def surface_table():
    spacing = np.linspace(-1.0, 1.0, EQ_ORDER)
    mesh_x, mesh_y, mesh_z = np.meshgrid(spacing, spacing, spacing, indexing="ij")
    lattice = np.stack([mesh_x.ravel(), mesh_y.ravel(), mesh_z.ravel()], 0)
    on_boundary = np.max(np.abs(lattice), axis=0) > 0.999
    return lattice[:, on_boundary] * 2.95


def split3(v):
    a = v.astype(BF16).astype(F32)
    r = v - a
    b = r.astype(BF16).astype(F32)
    return a, b, r - b


def source_features(p, row):
    nsq = jnp.sum(p * p, axis=0, keepdims=True)
    u = jnp.where(row == 3, nsq, jnp.where(row == 4, 1.0, p))
    a, b, c = split3(u)
    return jnp.concatenate([a, a, b, b, a, c], axis=0)


def target_features(t, row):
    nsq = jnp.sum(t * t, axis=0, keepdims=True) + SOFTEN
    v = jnp.where(row == 3, 1.0, jnp.where(row == 4, nsq, -2.0 * t))
    a, b, c = split3(v)
    return jnp.concatenate([a, b, a, b, c, a], axis=0).astype(BF16)


def surface_features():
    pts = np.zeros((8, FAR), np.float32)
    pts[:3, :S] = surface_table().astype(np.float32)
    pts[:3, S:] = pts[:3, :1]
    u = pts.copy()
    u[3] = np.sum(pts * pts, axis=0)
    u[4] = 1.0
    a = u.astype(jnp.bfloat16).astype(np.float32)
    b = (u - a).astype(jnp.bfloat16).astype(np.float32)
    c = u - a - b
    return np.ascontiguousarray(np.concatenate([a, a, b, b, a, c], axis=0).T)


def green(feat, ft):
    g = lax.rsqrt(jnp.dot(feat, ft, preferred_element_type=F32))
    hi = g.astype(BF16)
    return hi, (g - hi.astype(F32)).astype(BF16)


def pair_sum(feat, ft, weights):
    parts = []
    for at in range(0, PTS, 256):
        hi, lo = green(feat, ft[:, at : at + 256])
        parts.append(
            jnp.dot(weights, hi, preferred_element_type=F32)
            + jnp.dot(weights, lo, preferred_element_type=F32)
        )
    return jnp.concatenate(parts, axis=1)


def lane_of(shape):
    return lax.broadcasted_iota(jnp.int32, shape, 1)


def pack(v):
    end = v[:, 256:SP]
    last = jnp.concatenate([end[48:ROWS], jnp.zeros((8, 128), F32)], axis=0)
    shared = end[0:24] + pltpu.roll(end[24:48], TAIL, 1) + pltpu.roll(last, 2 * TAIL, 1)
    return jnp.concatenate([v[:, 0:128], v[:, 128:256], shared], axis=0)


def unpack(p):
    shared = p[2 * ROWS : PACKED]
    keep = lane_of((24, 128)) < TAIL
    ends = [jnp.where(keep, pltpu.roll(shared, (128 - TAIL * g) % 128, 1) if g else shared, 0.0) for g in range(3)]
    end = jnp.concatenate([ends[0], ends[1], ends[2][0:16]], axis=0)
    return jnp.concatenate([p[0:ROWS], p[ROWS : 2 * ROWS], end], axis=1)


def split2(v):
    hi = v.astype(BF16)
    return hi, (v - hi.astype(F32)).astype(BF16)


def dot3(x, w_hi, w_lo):
    hi, lo = split2(x)
    n = x.shape[0]
    both = jnp.concatenate([hi, lo], axis=0)
    r = jnp.dot(both, w_hi, preferred_element_type=F32)
    return r[:n] + r[n:] + jnp.dot(hi, w_lo, preferred_element_type=F32)


def kernel(
    octs, users, nears, codes, pts_in, ch_in, dens_in, up_in, low_in, upp_in, down_in, surf_in,
    out,
    pts, ch, dens, maps, surf, maps_hi, maps_lo, fsurf,
    xp, fs, cw, hp, hc, near, rbuf, p1, qb, p2, zb, gz, g2, wb, sbuf, vbuf, cfar, gh, gl,
    near_s, far_s, load_s, halo_s, halo_r, a_s, a_r, b_s, b_r, z_s, z_r,
    gz_s, gz_r, gb_s, gb_r, v_s, v_r,
):
    me = lax.axis_index("cube")
    count = 2 * NX * NY * NZ
    core = me % 2
    z = (me // 2) % NZ
    y = (me // (2 * NZ)) % NY
    x = me // (2 * NZ * NY)
    stride_x, stride_y = 2 * NZ * NY, 2 * NZ
    stride_a = stride_x * (1 - core) + stride_y * core
    stride_b = stride_y * (1 - core) + stride_x * core
    a = x * (1 - core) + y * core
    b = y * (1 - core) + x * core
    partner = me + 1 - 2 * core
    oct_a = core * (NG * NG * NZ) + a * (NG * NZ)

    def peer_a(i):
        return me + ((a + i) % NG - a) * stride_a

    def peer_b(i):
        return me + ((b + i) % NG - b) * stride_b

    def peer_z(i):
        return me + ((z + i) % NZ - z) * 2

    def cross_a(i):
        return peer_a(i) + 1 - 2 * core

    def cross_b(i):
        return peer_b(i) + 1 - 2 * core

    def far_first(t):
        return NZ // 2 + (t + 1) // 2 * (1 - 2 * (t % 2))

    def send(src, dst, s, r, dev):
        return pltpu.make_async_remote_copy(
            src_ref=src, dst_ref=dst, send_sem=s, recv_sem=r, device_id=(dev,), device_id_type=MESH
        )

    row8 = lax.broadcasted_iota(jnp.int32, (8, PTS), 0)

    barrier = pltpu.get_barrier_semaphore()

    def greet(dev):
        pl.semaphore_signal(barrier, inc=1, device_id=(dev,), device_id_type=MESH)

    greet(partner)
    for i in range(1, NG):
        greet(peer_a(i))
        greet(peer_b(i))
        greet(cross_a(i))
        greet(cross_b(i))

    z_near = (1, 2, NZ - 2, NZ - 1) if NZ == 16 else tuple(range(1, NZ))
    for i in z_near:
        greet(peer_z(i))
    n_greet = 1 + 4 * (NG - 1) + len(z_near)

    def tell(sem, reach):
        if NZ == 16:
            for i in (reach, NZ - reach):
                pl.semaphore_signal(sem, inc=1, device_id=(peer_z(i),), device_id_type=MESH)

    def step_near():
        if NZ == 16:
            pl.semaphore_wait(near_s, 2)
        tell(far_s, 4)

    def step_far():
        if NZ == 16:
            pl.semaphore_wait(far_s, 2)

    @pl.when(me > 0)
    def _():
        greet(me - 1)

    @pl.when(me < count - 1)
    def _():
        greet(me + 1)

    def load(i):
        src = (dens_in, pts_in, ch_in, surf_in, up_in, low_in, upp_in, down_in)[i]
        dst = (dens, pts, ch, surf, maps.at[0], maps.at[1], maps.at[2], maps.at[3])[i]
        return pltpu.make_async_copy(src, dst, load_s.at[i])

    for i in range(8):
        load(i).start()

    mine = a * 2 + core
    lane = lane_of((8, 128)) % ROWS
    keys = jnp.zeros((8, 128), jnp.int32)
    for l in range(LB):
        keys = jnp.where(lane // Q == l, octs[l], keys)
    rbuf[mine, PACKED : PACKED + 8, :] = (keys * Q + lane % Q).astype(F32)
    row24 = lax.broadcasted_iota(jnp.int32, (24, 128), 0)
    lane24 = lane_of((24, 128))
    column = jnp.zeros((24, 128), jnp.int32)
    for l in range(LB):
        here = jnp.logical_and(row24 // Q == l % 6, lane24 == 3 * TAIL + l // 6)
        column = jnp.where(here, octs[l] * Q + row24 % Q, column)
    g2[...] = jnp.zeros(g2.shape, F32)
    load(0).wait()
    for l in range(LB):
        g2[Q * l : Q * l + Q, 0:S] = dens[l]
    packed = pack(g2[0:ROWS])
    rbuf[mine, 0 : 2 * ROWS, :] = packed[0 : 2 * ROWS]
    rbuf[mine, 2 * ROWS : PACKED, :] = packed[2 * ROWS : PACKED] + column.astype(F32)

    def prep(n, p, q):
        fs[n] = source_features(p, row8).T.astype(BF16)
        hi = q.astype(BF16).astype(F32)
        cw[n] = jnp.concatenate([hi, q - hi, jnp.zeros((8, PTS), F32)], axis=0).astype(BF16)

    xp[...] = jnp.zeros(xp.shape, F32)
    load(1).wait()
    load(2).wait()

    def prep_own(n, _):
        for c in range(3):
            xp[n, c : c + 1, :] = pts[c, pl.ds(n, 1), :]
        prep(n, xp[n], ch[n] * INV_FOUR_PI)
        return 0

    lax.fori_loop(0, LB // 2, prep_own, 0, unroll=2)

    n_wait = n_greet + (me + count - 1) // count + (2 * count - 2 - me) // count
    pl.semaphore_wait(barrier, n_wait)

    def halo(i):
        dev = me + 1 - 2 * i
        return (
            send(pts_in, hp.at[i], halo_s.at[i], halo_r.at[i], dev),
            send(ch_in, hc.at[i], halo_s.at[2 + i], halo_r.at[2 + i], dev),
        )

    def a_copy(i, slot):
        dev = peer_a(i) if i < NG else cross_b(i - NG)
        return send(rbuf.at[mine], rbuf.at[slot], a_s.at[i], a_r.at[i], dev)

    def a_send(i):
        return a_copy(i, mine if i < NG else b * 2 + core)

    def a_take(i):
        return a_copy(i, (a + 2 * NG - i) % NG * 2 + (core if i < NG else 1 - core))

    a_all = tuple(range(1, 2 * NG))

    def b_copy(i, chunk, at):
        return send(p1.at[pl.ds(chunk * NZ * Q, NZ * Q)], qb.at[at], b_s.at[i], b_r.at[i], peer_b(i))

    def z_copy(i, chunk, at):
        return send(p2.at[chunk], zb.at[at], z_s.at[i], z_r.at[i], peer_z(i))

    def gz_copy(i, at):
        return send(gz.at[at], gz.at[at], gz_s.at[i], gz_r.at[i], peer_z(i))

    def gb_copy(i, at):
        return send(wb.at[at], wb.at[at], gb_s.at[i], gb_r.at[i], peer_b(i))

    def v_copy(i, at):
        dev = peer_a(i) if i < NG else cross_a(i - NG)
        slot = (a + i) % NG * 2 + (core if i < NG else 1 - core)
        return send(sbuf.at[slot], vbuf.at[at], v_s.at[i], v_r.at[i], dev)

    def v_send(i):
        return v_copy(i, a if i < NG else NG + a)

    def v_place(i):
        return (a + NG - i) % NG if i < NG else NG + (b + 2 * NG - i) % NG

    for i in a_all:
        a_send(i).start()
    tell(near_s, 2)

    @pl.when(me < count - 1)
    def _():
        for c in halo(0):
            c.start()

    @pl.when(me > 0)
    def _():
        for c in halo(1):
            c.start()

    def step_b():
        for i in a_all:
            a_take(i).wait_recv()
        rows = lax.broadcasted_iota(jnp.int32, (NG * NZ * Q, 3 * ROWS), 0) + oct_a * Q
        rows = rows.astype(F32)

        def add(j, _):
            key = rbuf[j, PACKED : PACKED + 1, :]
            key = jnp.concatenate([key, key[:, 0:ROWS]], axis=1)
            member = jnp.where(rows == key, 1.0, 0.0).astype(BF16)
            parts = jnp.concatenate(split3(unpack(rbuf[j, 0:PACKED, :])), axis=0).astype(BF16)
            p1[...] += jnp.dot(member, parts, preferred_element_type=F32)
            return 0

        p1[...] = jnp.zeros(p1.shape, F32)
        lax.fori_loop(0, 2 * NG, add, 0)
        for i in range(1, NG):
            b_copy(i, (b + i) % NG, b).start()

    def step_z():
        total = p1[pl.ds(pl.multiple_of(b * NZ * Q, 8), NZ * Q), :]
        for i in range(1, NG):
            at = (b + NG - i) % NG
            b_copy(i, at, at).wait_recv()
            total = total + qb[at]
        for j in range(NZ):
            p2[j] = total[Q * j : Q * j + Q, :]

        def go(t, _):
            i = far_first(t)
            z_copy(i, (z + i) % NZ, z).start()
            return 0

        lax.fori_loop(0, NZ - 1, go, 0)

    def step_gz():
        def take(i, total):
            at = (z + NZ - i) % NZ
            z_copy(i, at, at).wait_recv()
            return total + zb[at]

        gz[z] = lax.fori_loop(1, NZ, take, p2[z])

        def go(t, _):
            gz_copy(far_first(t), z).start()
            return 0

        lax.fori_loop(0, NZ - 1, go, 0)

    def step_gb():
        def take(i, _):
            gz_copy(i, (z + NZ - i) % NZ).wait_recv()
            return 0

        lax.fori_loop(1, NZ, take, 0)
        for j in range(NZ):
            g2[Q * j : Q * j + Q, :] = gz[j]
        e = dot3(g2[0 : NZ * Q, 0:S], maps_hi[0], maps_lo[0])
        none = jnp.zeros((8, S), F32)
        w = jnp.concatenate([none, dot3(e, maps_hi[1], maps_lo[1])], axis=0) + jnp.concatenate(
            [dot3(e, maps_hi[2], maps_lo[2]), none], axis=0
        )
        wb[b] = jnp.zeros(wb.shape[1:], F32)
        wb[b, :, 0:S] = dot3(w, maps_hi[3], maps_lo[3]) * INV_FOUR_PI
        for i in range(1, NG):
            gb_copy(i, b).start()

    def step_v():
        for i in range(1, NG):
            gb_copy(i, (b + NG - i) % NG).wait_recv()
        ext = NZ * Q + 8
        cols = lax.broadcasted_iota(jnp.int32, (2 * ROWS, NG * ext), 1)
        cols = cols % ext + (cols // ext) * (NZ * Q) + (oct_a - 1) * Q
        cols = cols.astype(F32)
        hi, lo = split2(wb[...].reshape(NG * ext, SP))
        for i in list(range(1, NG)) + [0]:
            at = (a + i) % NG
            key = []
            for h in range(2):
                shared = rbuf[at * 2 + h, 2 * ROWS : PACKED, :]
                for g, n in enumerate((24, 24, 16)):
                    key.append(shared[0:n, 3 * TAIL + g : 3 * TAIL + g + 1])
            key = jnp.concatenate(key, axis=0)
            member = jnp.where(cols == key, 1.0, 0.0).astype(BF16)
            picked = jnp.dot(member, hi, preferred_element_type=F32) + jnp.dot(
                member, lo, preferred_element_type=F32
            )
            for h in range(2):
                sbuf[at * 2 + h] = pack(picked[h * ROWS : h * ROWS + ROWS])
            if i > 0:
                v_send(i).start()
            v_send(NG + i).start()

    steps = (step_near, step_far, step_b, step_z, step_gz, step_gb, step_v)

    def run_steps(at):
        for place, step in zip(STEP_AT, steps):

            @pl.when(at == place)
            def _():
                step()

    lax.fori_loop(LB // 2, LB, prep_own, 0, unroll=2)
    for i in range(3, 8):
        load(i).wait()
    fsurf[...] = surf[...].astype(BF16)
    for i in range(4):
        maps_hi[i], maps_lo[i] = split2(maps[i])

    def own_pair(t, _):
        for h in range(2):
            l = 2 * t + h
            near[l] = pair_sum(fs[l], target_features(xp[l], row8), cw[l])
        run_steps(2 * t)
        return 0

    lax.fori_loop(0, LB // 2, own_pair, 0)

    for i in range(2):
        present = me > 0 if i == 0 else me < count - 1

        @pl.when(present)
        def _():
            for c in halo(i):
                c.wait_recv()

        @pl.when(jnp.logical_not(present))
        def _():
            hp[i] = jnp.zeros(hp.shape[1:], F32)
            hc[i] = jnp.zeros(hc.shape[1:], F32)

    for i in range(2):

        def prep_halo(j, _):
            n = users[i, j]
            at = LB + i * UH + j
            for c in range(3):
                xp[at, c : c + 1, :] = hp[i, c, pl.ds(n, 1), :]
            prep(at, xp[at], hc[i, n] * INV_FOUR_PI)
            return 0

        lax.fori_loop(0, UH, prep_halo, 0, unroll=2)

    def near_leaf(l, _):
        acc = near[l]
        box = xp[l]
        for k in range(K):
            n = nears[k, l]
            code = codes[k, l]
            code = jnp.where(code >= 13, code + 1, code)
            ox = (2 * (code // 9 - 1)).astype(F32)
            oy = (2 * ((code // 3) % 3 - 1)).astype(F32)
            oz = (2 * (code % 3 - 1)).astype(F32)
            off = jnp.where(row8 == 0, ox, jnp.where(row8 == 1, oy, jnp.where(row8 == 2, oz, 0.0)))
            acc = acc + pair_sum(fs[n], target_features(box - off, row8), cw[n])
        near[l] = acc
        run_steps(LB + l)
        return 0

    lax.fori_loop(0, LB, near_leaf, 0)

    def far_some(t, _):
        for h in range(4):
            l = 4 * t + h
            gh[l], gl[l] = green(fsurf[...], target_features(xp[l], row8))
        run_steps(2 * LB + 4 * t)
        return 0

    lax.fori_loop(0, LB // 4, far_some, 0)

    w = sbuf[mine]
    for i in a_all:
        v_copy(i, v_place(i)).wait_recv()
        w = w + vbuf[v_place(i)]
    w = unpack(w)
    hi = w.astype(BF16).astype(F32)
    lo = w - hi
    for t in range(LB // 2):
        pair = jnp.concatenate([hi[8 * t : 8 * t + 8], lo[8 * t : 8 * t + 8]], axis=0)
        cfar[t] = pair.astype(BF16)

    def far_pair(t, _):
        for h in range(2):
            l = 2 * t + h
            c = cfar[t, :, 0:FAR]
            far = jnp.dot(c, gh[l], preferred_element_type=F32) + jnp.dot(
                c, gl[l], preferred_element_type=F32
            )
            far = far[0:8] + far[8:16]
            out[l] = far[4 * h : 4 * h + 4] + near[l, 0:4, :] + near[l, 4:8, :]
        return 0

    lax.fori_loop(0, LB // 2, far_pair, 0, unroll=2)

    for i in a_all:
        a_send(i).wait_send()
        v_send(i).wait_send()

    @pl.when(me < count - 1)
    def _():
        for c in halo(0):
            c.wait_send()

    @pl.when(me > 0)
    def _():
        for c in halo(1):
            c.wait_send()

    for i in range(1, NG):
        b_copy(i, (b + i) % NG, b).wait_send()
        gb_copy(i, b).wait_send()

    def sent_z(i, _):
        z_copy(i, (z + i) % NZ, z).wait_send()
        gz_copy(i, z).wait_send()
        return 0

    lax.fori_loop(1, NZ, sent_z, 0)


STEP_AT = (0, 6, 14, 18, 23, 29, 36)


def body(points, charges, leaf_density, leaf_octant, user_lists, near_leaves, near_codes,
         upward_map, lower_map, upper_map, downward_map):
    smem = pl.BlockSpec(memory_space=pltpu.SMEM)
    hbm = pl.BlockSpec(memory_space=pltpu.HBM)
    dma = pltpu.SemaphoreType.DMA
    return pl.pallas_call(
        kernel,
        out_shape=jax.ShapeDtypeStruct((LB, Q, PTS), F32),
        in_specs=[smem] * 4 + [hbm] * 8,
        out_specs=pl.BlockSpec(memory_space=pltpu.VMEM),
        scratch_shapes=[
            pltpu.VMEM((3, LB, PTS), F32),
            pltpu.VMEM((LB, Q, PTS), F32),
            pltpu.VMEM((LB, Q, S), F32),
            pltpu.VMEM((4, S, S), F32),
            pltpu.VMEM((FAR, 48), F32),
            pltpu.VMEM((4, S, S), BF16),
            pltpu.VMEM((4, S, S), BF16),
            pltpu.VMEM((FAR, 48), BF16),
            pltpu.VMEM((LB + 2 * UH, 8, PTS), F32),
            pltpu.VMEM((LB + 2 * UH, PTS, 48), BF16),
            pltpu.VMEM((LB + 2 * UH, 16, PTS), BF16),
            pltpu.VMEM((2, 3, LB, PTS), F32),
            pltpu.VMEM((2, LB, Q, PTS), F32),
            pltpu.VMEM((LB, 16, PTS), F32),
            pltpu.VMEM((2 * NG, PACKED + 8, 128), F32),
            pltpu.VMEM((NG * NZ * Q, SP), F32),
            pltpu.VMEM((NG, NZ * Q, SP), F32),
            pltpu.VMEM((NZ, Q, SP), F32),
            pltpu.VMEM((NZ, Q, SP), F32),
            pltpu.VMEM((NZ, Q, SP), F32),
            pltpu.VMEM((max(NZ * Q, ROWS), SP), F32),
            pltpu.VMEM((NG, NZ * Q + 8, SP), F32),
            pltpu.VMEM((2 * NG, PACKED, 128), F32),
            pltpu.VMEM((2 * NG, PACKED, 128), F32),
            pltpu.VMEM((LB // 2, 16, SP), BF16),
            pltpu.VMEM((LB, FAR, PTS), BF16),
            pltpu.VMEM((LB, FAR, PTS), BF16),
            pltpu.SemaphoreType.REGULAR, pltpu.SemaphoreType.REGULAR,
            dma((8,)), dma((4,)), dma((4,)), dma((2 * NG,)), dma((2 * NG,)),
            dma((NG,)), dma((NG,)), dma((NZ,)), dma((NZ,)), dma((NZ,)), dma((NZ,)),
            dma((NG,)), dma((NG,)), dma((2 * NG,)), dma((2 * NG,)),
        ],
        compiler_params=pltpu.CompilerParams(
            collective_id=0, has_side_effects=True, vmem_limit_bytes=56 * 2**20
        ),
    )(
        leaf_octant, user_lists.reshape(2, UH), near_leaves.T, near_codes.T,
        points.transpose(1, 0, 2), charges, leaf_density,
        upward_map, lower_map, upper_map, downward_map, jnp.asarray(surface_features(), F32),
    )


def solution(mesh):
    in_specs = (
        P("cube", None, None),
        P("cube", None, None),
        P("cube", None, None),
        P("cube"),
        P("cube", None, None),
        P("cube", None),
        P("cube", None),
        P(),
        P(),
        P(),
        P(),
    )
    return jax.shard_map(
        body, mesh=mesh, in_specs=in_specs, out_specs=P("cube", None, None), check_vma=False
    )
```

```python
import functools
import math

import jax
import jax.numpy as jnp
import numpy as np
from jax import lax
from jax.experimental import pallas as pl
from jax.experimental.pallas import tpu as pltpu
from jax.sharding import PartitionSpec as P

EQ_ORDER = 8
INV_FOUR_PI = 1.0 / (4.0 * math.pi)
SOFTEN = 0.01
LB = 16
UH = 4
K = 4
Q = 4
S = 296
SP = 384
PTS = 512
FAR = 304
ROWS = LB * Q
TAIL = S - 256
PACKED = 2 * ROWS + 24
MESH = pl.DeviceIdType.MESH
F32 = jnp.float32
BF16 = jnp.bfloat16
NX, NY, NZ = 4, 4, 16
NG = 4


def surface_table():
    spacing = np.linspace(-1.0, 1.0, EQ_ORDER)
    mesh_x, mesh_y, mesh_z = np.meshgrid(spacing, spacing, spacing, indexing="ij")
    lattice = np.stack([mesh_x.ravel(), mesh_y.ravel(), mesh_z.ravel()], 0)
    on_boundary = np.max(np.abs(lattice), axis=0) > 0.999
    return lattice[:, on_boundary] * 2.95


def split3(v):
    a = v.astype(BF16).astype(F32)
    r = v - a
    b = r.astype(BF16).astype(F32)
    return a, b, r - b


def source_features(p, row):
    nsq = jnp.sum(p * p, axis=0, keepdims=True)
    u = jnp.where(row == 3, nsq, jnp.where(row == 4, 1.0, p))
    a, b, c = split3(u)
    return jnp.concatenate([a, a, b, b, a, c], axis=0)


def target_features(t, row):
    nsq = jnp.sum(t * t, axis=0, keepdims=True) + SOFTEN
    v = jnp.where(row == 3, 1.0, jnp.where(row == 4, nsq, -2.0 * t))
    a, b, c = split3(v)
    return jnp.concatenate([a, b, a, b, c, a], axis=0).astype(BF16)


def surface_features():
    pts = np.zeros((8, FAR), np.float32)
    pts[:3, :S] = surface_table().astype(np.float32)
    pts[:3, S:] = pts[:3, :1]
    u = pts.copy()
    u[3] = np.sum(pts * pts, axis=0)
    u[4] = 1.0
    a = u.astype(jnp.bfloat16).astype(np.float32)
    b = (u - a).astype(jnp.bfloat16).astype(np.float32)
    c = u - a - b
    return np.ascontiguousarray(np.concatenate([a, a, b, b, a, c], axis=0).T)


def green(feat, ft):
    g = lax.rsqrt(jnp.dot(feat, ft, preferred_element_type=F32))
    hi = g.astype(BF16)
    return hi, (g - hi.astype(F32)).astype(BF16)


def pair_sum(feat, ft, weights):
    parts = []
    for at in range(0, PTS, 256):
        hi, lo = green(feat, ft[:, at : at + 256])
        parts.append(
            jnp.dot(weights, hi, preferred_element_type=F32)
            + jnp.dot(weights, lo, preferred_element_type=F32)
        )
    return jnp.concatenate(parts, axis=1)


def lane_of(shape):
    return lax.broadcasted_iota(jnp.int32, shape, 1)


def pack(v):
    end = v[:, 256:SP]
    last = jnp.concatenate([end[48:ROWS], jnp.zeros((8, 128), F32)], axis=0)
    shared = end[0:24] + pltpu.roll(end[24:48], TAIL, 1) + pltpu.roll(last, 2 * TAIL, 1)
    return jnp.concatenate([v[:, 0:128], v[:, 128:256], shared], axis=0)


def unpack(p):
    shared = p[2 * ROWS : PACKED]
    keep = lane_of((24, 128)) < TAIL
    ends = [jnp.where(keep, pltpu.roll(shared, (128 - TAIL * g) % 128, 1) if g else shared, 0.0) for g in range(3)]
    end = jnp.concatenate([ends[0], ends[1], ends[2][0:16]], axis=0)
    return jnp.concatenate([p[0:ROWS], p[ROWS : 2 * ROWS], end], axis=1)


def split2(v):
    hi = v.astype(BF16)
    return hi, (v - hi.astype(F32)).astype(BF16)


def dot3(x, w_hi, w_lo):
    hi, lo = split2(x)
    n = x.shape[0]
    both = jnp.concatenate([hi, lo], axis=0)
    r = jnp.dot(both, w_hi, preferred_element_type=F32)
    return r[:n] + r[n:] + jnp.dot(hi, w_lo, preferred_element_type=F32)


def kernel(
    octs, users, nears, codes, pts_in, ch_in, dens_in, up_in, low_in, upp_in, down_in, surf_in,
    out,
    pts, ch, dens, maps, surf, maps_hi, maps_lo, fsurf,
    xp, fs, cw, hp, hc, near, rbuf, p1, qb, p2, zb, gz, g2, wb, sbuf, vbuf, cfar, gh, gl,
    near_s, far_s, load_s, halo_s, halo_r, a_s, a_r, b_s, b_r, z_s, z_r,
    gz_s, gz_r, gb_s, gb_r, v_s, v_r,
):
    me = lax.axis_index("cube")
    count = 2 * NX * NY * NZ
    core = me % 2
    z = (me // 2) % NZ
    y = (me // (2 * NZ)) % NY
    x = me // (2 * NZ * NY)
    stride_x, stride_y = 2 * NZ * NY, 2 * NZ
    stride_a = stride_x * (1 - core) + stride_y * core
    stride_b = stride_y * (1 - core) + stride_x * core
    a = x * (1 - core) + y * core
    b = y * (1 - core) + x * core
    partner = me + 1 - 2 * core
    oct_a = core * (NG * NG * NZ) + a * (NG * NZ)

    def peer_a(i):
        return me + ((a + i) % NG - a) * stride_a

    def peer_b(i):
        return me + ((b + i) % NG - b) * stride_b

    def peer_z(i):
        return me + ((z + i) % NZ - z) * 2

    def cross_a(i):
        return peer_a(i) + 1 - 2 * core

    def cross_b(i):
        return peer_b(i) + 1 - 2 * core

    def far_first(t):
        return NZ // 2 + (t + 1) // 2 * (1 - 2 * (t % 2))

    def send(src, dst, s, r, dev):
        return pltpu.make_async_remote_copy(
            src_ref=src, dst_ref=dst, send_sem=s, recv_sem=r, device_id=(dev,), device_id_type=MESH
        )

    row8 = lax.broadcasted_iota(jnp.int32, (8, PTS), 0)

    barrier = pltpu.get_barrier_semaphore()

    def greet(dev):
        pl.semaphore_signal(barrier, inc=1, device_id=(dev,), device_id_type=MESH)

    greet(partner)
    for i in range(1, NG):
        greet(peer_a(i))
        greet(peer_b(i))
        greet(cross_a(i))
        greet(cross_b(i))

    z_near = (1, 2, NZ - 2, NZ - 1) if NZ == 16 else tuple(range(1, NZ))
    for i in z_near:
        greet(peer_z(i))
    n_greet = 1 + 4 * (NG - 1) + len(z_near)

    def tell(sem, reach):
        if NZ == 16:
            for i in (reach, NZ - reach):
                pl.semaphore_signal(sem, inc=1, device_id=(peer_z(i),), device_id_type=MESH)

    def step_near():
        if NZ == 16:
            pl.semaphore_wait(near_s, 2)
        tell(far_s, 4)

    def step_far():
        if NZ == 16:
            pl.semaphore_wait(far_s, 2)

    @pl.when(me > 0)
    def _():
        greet(me - 1)

    @pl.when(me < count - 1)
    def _():
        greet(me + 1)

    def load(i):
        src = (dens_in, pts_in, ch_in, surf_in, up_in, low_in, upp_in, down_in)[i]
        dst = (dens, pts, ch, surf, maps.at[0], maps.at[1], maps.at[2], maps.at[3])[i]
        return pltpu.make_async_copy(src, dst, load_s.at[i])

    for i in range(8):
        load(i).start()

    mine = a * 2 + core
    lane = lane_of((8, 128)) % ROWS
    keys = jnp.zeros((8, 128), jnp.int32)
    for l in range(LB):
        keys = jnp.where(lane // Q == l, octs[l], keys)
    rbuf[mine, PACKED : PACKED + 8, :] = (keys * Q + lane % Q).astype(F32)
    row24 = lax.broadcasted_iota(jnp.int32, (24, 128), 0)
    lane24 = lane_of((24, 128))
    column = jnp.zeros((24, 128), jnp.int32)
    for l in range(LB):
        here = jnp.logical_and(row24 // Q == l % 6, lane24 == 3 * TAIL + l // 6)
        column = jnp.where(here, octs[l] * Q + row24 % Q, column)
    g2[...] = jnp.zeros(g2.shape, F32)
    load(0).wait()
    for l in range(LB):
        g2[Q * l : Q * l + Q, 0:S] = dens[l]
    packed = pack(g2[0:ROWS])
    rbuf[mine, 0 : 2 * ROWS, :] = packed[0 : 2 * ROWS]
    rbuf[mine, 2 * ROWS : PACKED, :] = packed[2 * ROWS : PACKED] + column.astype(F32)

    def prep(n, p, q):
        fs[n] = source_features(p, row8).T.astype(BF16)
        hi = q.astype(BF16).astype(F32)
        cw[n] = jnp.concatenate([hi, q - hi, jnp.zeros((8, PTS), F32)], axis=0).astype(BF16)

    xp[...] = jnp.zeros(xp.shape, F32)
    load(1).wait()
    load(2).wait()

    def prep_own(n, _):
        for c in range(3):
            xp[n, c : c + 1, :] = pts[c, pl.ds(n, 1), :]
        prep(n, xp[n], ch[n] * INV_FOUR_PI)
        return 0

    lax.fori_loop(0, LB // 2, prep_own, 0, unroll=4)

    n_wait = n_greet + (me + count - 1) // count + (2 * count - 2 - me) // count
    pl.semaphore_wait(barrier, n_wait)

    def halo(i):
        dev = me + 1 - 2 * i
        return (
            send(pts_in, hp.at[i], halo_s.at[i], halo_r.at[i], dev),
            send(ch_in, hc.at[i], halo_s.at[2 + i], halo_r.at[2 + i], dev),
        )

    def a_copy(i, slot):
        dev = peer_a(i) if i < NG else cross_b(i - NG)
        return send(rbuf.at[mine], rbuf.at[slot], a_s.at[i], a_r.at[i], dev)

    def a_send(i):
        return a_copy(i, mine if i < NG else b * 2 + core)

    def a_take(i):
        return a_copy(i, (a + 2 * NG - i) % NG * 2 + (core if i < NG else 1 - core))

    a_all = tuple(range(1, 2 * NG))

    def b_copy(i, chunk, at):
        return send(p1.at[pl.ds(chunk * NZ * Q, NZ * Q)], qb.at[at], b_s.at[i], b_r.at[i], peer_b(i))

    def z_copy(i, chunk, at):
        return send(p2.at[chunk], zb.at[at], z_s.at[i], z_r.at[i], peer_z(i))

    def gz_copy(i, at):
        return send(gz.at[at], gz.at[at], gz_s.at[i], gz_r.at[i], peer_z(i))

    def gb_copy(i, at):
        return send(wb.at[at], wb.at[at], gb_s.at[i], gb_r.at[i], peer_b(i))

    def v_copy(i, at):
        dev = peer_a(i) if i < NG else cross_a(i - NG)
        slot = (a + i) % NG * 2 + (core if i < NG else 1 - core)
        return send(sbuf.at[slot], vbuf.at[at], v_s.at[i], v_r.at[i], dev)

    def v_send(i):
        return v_copy(i, a if i < NG else NG + a)

    def v_place(i):
        return (a + NG - i) % NG if i < NG else NG + (b + 2 * NG - i) % NG

    for i in a_all:
        a_send(i).start()
    tell(near_s, 2)

    @pl.when(me < count - 1)
    def _():
        for c in halo(0):
            c.start()

    @pl.when(me > 0)
    def _():
        for c in halo(1):
            c.start()

    def step_b():
        for i in a_all:
            a_take(i).wait_recv()
        rows = lax.broadcasted_iota(jnp.int32, (NG * NZ * Q, 3 * ROWS), 0) + oct_a * Q
        rows = rows.astype(F32)

        def add(j, _):
            key = rbuf[j, PACKED : PACKED + 1, :]
            key = jnp.concatenate([key, key[:, 0:ROWS]], axis=1)
            member = jnp.where(rows == key, 1.0, 0.0).astype(BF16)
            parts = jnp.concatenate(split3(unpack(rbuf[j, 0:PACKED, :])), axis=0).astype(BF16)
            p1[...] += jnp.dot(member, parts, preferred_element_type=F32)
            return 0

        p1[...] = jnp.zeros(p1.shape, F32)
        lax.fori_loop(0, 2 * NG, add, 0)
        for i in range(1, NG):
            b_copy(i, (b + i) % NG, b).start()

    def step_z():
        total = p1[pl.ds(pl.multiple_of(b * NZ * Q, 8), NZ * Q), :]
        for i in range(1, NG):
            at = (b + NG - i) % NG
            b_copy(i, at, at).wait_recv()
            total = total + qb[at]
        for j in range(NZ):
            p2[j] = total[Q * j : Q * j + Q, :]

        def go(t, _):
            i = far_first(t)
            z_copy(i, (z + i) % NZ, z).start()
            return 0

        lax.fori_loop(0, NZ - 1, go, 0)

    def step_gz():
        def take(i, total):
            at = (z + NZ - i) % NZ
            z_copy(i, at, at).wait_recv()
            return total + zb[at]

        gz[z] = lax.fori_loop(1, NZ, take, p2[z])

        def go(t, _):
            gz_copy(far_first(t), z).start()
            return 0

        lax.fori_loop(0, NZ - 1, go, 0)

    def step_gb():
        def take(i, _):
            gz_copy(i, (z + NZ - i) % NZ).wait_recv()
            return 0

        lax.fori_loop(1, NZ, take, 0)
        for j in range(NZ):
            g2[Q * j : Q * j + Q, :] = gz[j]
        e = dot3(g2[0 : NZ * Q, 0:S], maps_hi[0], maps_lo[0])
        none = jnp.zeros((8, S), F32)
        w = jnp.concatenate([none, dot3(e, maps_hi[1], maps_lo[1])], axis=0) + jnp.concatenate(
            [dot3(e, maps_hi[2], maps_lo[2]), none], axis=0
        )
        wb[b] = jnp.zeros(wb.shape[1:], F32)
        wb[b, :, 0:S] = dot3(w, maps_hi[3], maps_lo[3]) * INV_FOUR_PI
        for i in range(1, NG):
            gb_copy(i, b).start()

    def step_v():
        for i in range(1, NG):
            gb_copy(i, (b + NG - i) % NG).wait_recv()
        ext = NZ * Q + 8
        cols = lax.broadcasted_iota(jnp.int32, (2 * ROWS, NG * ext), 1)
        cols = cols % ext + (cols // ext) * (NZ * Q) + (oct_a - 1) * Q
        cols = cols.astype(F32)
        hi, lo = split2(wb[...].reshape(NG * ext, SP))
        for i in list(range(1, NG)) + [0]:
            at = (a + i) % NG
            key = []
            for h in range(2):
                shared = rbuf[at * 2 + h, 2 * ROWS : PACKED, :]
                for g, n in enumerate((24, 24, 16)):
                    key.append(shared[0:n, 3 * TAIL + g : 3 * TAIL + g + 1])
            key = jnp.concatenate(key, axis=0)
            member = jnp.where(cols == key, 1.0, 0.0).astype(BF16)
            picked = jnp.dot(member, hi, preferred_element_type=F32) + jnp.dot(
                member, lo, preferred_element_type=F32
            )
            for h in range(2):
                sbuf[at * 2 + h] = pack(picked[h * ROWS : h * ROWS + ROWS])
            if i > 0:
                v_send(i).start()
            v_send(NG + i).start()

    steps = (step_near, step_far, step_b, step_z, step_gz, step_gb, step_v)

    def run_steps(at):
        for place, step in zip(STEP_AT, steps):

            @pl.when(at == place)
            def _():
                step()

    lax.fori_loop(LB // 2, LB, prep_own, 0, unroll=4)
    for i in range(3, 8):
        load(i).wait()
    fsurf[...] = surf[...].astype(BF16)
    for i in range(4):
        maps_hi[i], maps_lo[i] = split2(maps[i])

    def own_four(t, _):
        for h in range(4):
            l = 4 * t + h
            near[l] = pair_sum(fs[l], target_features(xp[l], row8), cw[l])
        run_steps(4 * t)
        return 0

    lax.fori_loop(0, LB // 4, own_four, 0)

    for i in range(2):
        present = me > 0 if i == 0 else me < count - 1

        @pl.when(present)
        def _():
            for c in halo(i):
                c.wait_recv()

        @pl.when(jnp.logical_not(present))
        def _():
            hp[i] = jnp.zeros(hp.shape[1:], F32)
            hc[i] = jnp.zeros(hc.shape[1:], F32)

    for i in range(2):

        def prep_halo(j, _):
            n = users[i, j]
            at = LB + i * UH + j
            for c in range(3):
                xp[at, c : c + 1, :] = hp[i, c, pl.ds(n, 1), :]
            prep(at, xp[at], hc[i, n] * INV_FOUR_PI)
            return 0

        lax.fori_loop(0, UH, prep_halo, 0, unroll=True)

    def near_leaf(l, _):
        acc = near[l]
        box = xp[l]
        for k in range(K):
            n = nears[k, l]
            code = codes[k, l]
            code = jnp.where(code >= 13, code + 1, code)
            ox = (2 * (code // 9 - 1)).astype(F32)
            oy = (2 * ((code // 3) % 3 - 1)).astype(F32)
            oz = (2 * (code % 3 - 1)).astype(F32)
            off = jnp.where(row8 == 0, ox, jnp.where(row8 == 1, oy, jnp.where(row8 == 2, oz, 0.0)))
            acc = acc + pair_sum(fs[n], target_features(box - off, row8), cw[n])
        near[l] = acc
        run_steps(LB + l)
        return 0

    lax.fori_loop(0, LB, near_leaf, 0)

    def far_some(t, _):
        for h in range(4):
            l = 4 * t + h
            gh[l], gl[l] = green(fsurf[...], target_features(xp[l], row8))
        run_steps(2 * LB + 4 * t)
        return 0

    lax.fori_loop(0, LB // 4, far_some, 0)

    w = sbuf[mine]
    for i in a_all:
        v_copy(i, v_place(i)).wait_recv()
        w = w + vbuf[v_place(i)]
    w = unpack(w)
    hi = w.astype(BF16).astype(F32)
    lo = w - hi
    for t in range(LB // 2):
        pair = jnp.concatenate([hi[8 * t : 8 * t + 8], lo[8 * t : 8 * t + 8]], axis=0)
        cfar[t] = pair.astype(BF16)

    def far_pair(t, _):
        for h in range(2):
            l = 2 * t + h
            c = cfar[t, :, 0:FAR]
            far = jnp.dot(c, gh[l], preferred_element_type=F32) + jnp.dot(
                c, gl[l], preferred_element_type=F32
            )
            far = far[0:8] + far[8:16]
            out[l] = far[4 * h : 4 * h + 4] + near[l, 0:4, :] + near[l, 4:8, :]
        return 0

    lax.fori_loop(0, LB // 2, far_pair, 0, unroll=2)

    for i in a_all:
        a_send(i).wait_send()
        v_send(i).wait_send()

    @pl.when(me < count - 1)
    def _():
        for c in halo(0):
            c.wait_send()

    @pl.when(me > 0)
    def _():
        for c in halo(1):
            c.wait_send()

    for i in range(1, NG):
        b_copy(i, (b + i) % NG, b).wait_send()
        gb_copy(i, b).wait_send()

    def sent_z(i, _):
        z_copy(i, (z + i) % NZ, z).wait_send()
        gz_copy(i, z).wait_send()
        return 0

    lax.fori_loop(1, NZ, sent_z, 0)


STEP_AT = (0, 8, 12, 18, 23, 29, 36)


def body(points, charges, leaf_density, leaf_octant, user_lists, near_leaves, near_codes,
         upward_map, lower_map, upper_map, downward_map):
    smem = pl.BlockSpec(memory_space=pltpu.SMEM)
    hbm = pl.BlockSpec(memory_space=pltpu.HBM)
    dma = pltpu.SemaphoreType.DMA
    return pl.pallas_call(
        kernel,
        out_shape=jax.ShapeDtypeStruct((LB, Q, PTS), F32),
        in_specs=[smem] * 4 + [hbm] * 8,
        out_specs=pl.BlockSpec(memory_space=pltpu.VMEM),
        scratch_shapes=[
            pltpu.VMEM((3, LB, PTS), F32),
            pltpu.VMEM((LB, Q, PTS), F32),
            pltpu.VMEM((LB, Q, S), F32),
            pltpu.VMEM((4, S, S), F32),
            pltpu.VMEM((FAR, 48), F32),
            pltpu.VMEM((4, S, S), BF16),
            pltpu.VMEM((4, S, S), BF16),
            pltpu.VMEM((FAR, 48), BF16),
            pltpu.VMEM((LB + 2 * UH, 8, PTS), F32),
            pltpu.VMEM((LB + 2 * UH, PTS, 48), BF16),
            pltpu.VMEM((LB + 2 * UH, 16, PTS), BF16),
            pltpu.VMEM((2, 3, LB, PTS), F32),
            pltpu.VMEM((2, LB, Q, PTS), F32),
            pltpu.VMEM((LB, 16, PTS), F32),
            pltpu.VMEM((2 * NG, PACKED + 8, 128), F32),
            pltpu.VMEM((NG * NZ * Q, SP), F32),
            pltpu.VMEM((NG, NZ * Q, SP), F32),
            pltpu.VMEM((NZ, Q, SP), F32),
            pltpu.VMEM((NZ, Q, SP), F32),
            pltpu.VMEM((NZ, Q, SP), F32),
            pltpu.VMEM((max(NZ * Q, ROWS), SP), F32),
            pltpu.VMEM((NG, NZ * Q + 8, SP), F32),
            pltpu.VMEM((2 * NG, PACKED, 128), F32),
            pltpu.VMEM((2 * NG, PACKED, 128), F32),
            pltpu.VMEM((LB // 2, 16, SP), BF16),
            pltpu.VMEM((LB, FAR, PTS), BF16),
            pltpu.VMEM((LB, FAR, PTS), BF16),
            pltpu.SemaphoreType.REGULAR, pltpu.SemaphoreType.REGULAR,
            dma((8,)), dma((4,)), dma((4,)), dma((2 * NG,)), dma((2 * NG,)),
            dma((NG,)), dma((NG,)), dma((NZ,)), dma((NZ,)), dma((NZ,)), dma((NZ,)),
            dma((NG,)), dma((NG,)), dma((2 * NG,)), dma((2 * NG,)),
        ],
        compiler_params=pltpu.CompilerParams(
            collective_id=0, has_side_effects=True, vmem_limit_bytes=56 * 2**20
        ),
    )(
        leaf_octant, user_lists.reshape(2, UH), near_leaves.T, near_codes.T,
        points.transpose(1, 0, 2), charges, leaf_density,
        upward_map, lower_map, upper_map, downward_map, jnp.asarray(surface_features(), F32),
    )


def solution(mesh):
    in_specs = (
        P("cube", None, None),
        P("cube", None, None),
        P("cube", None, None),
        P("cube"),
        P("cube", None, None),
        P("cube", None),
        P("cube", None),
        P(),
        P(),
        P(),
        P(),
    )
    return jax.shard_map(
        body, mesh=mesh, in_specs=in_specs, out_specs=P("cube", None, None), check_vma=False
    )
```
